1024 devices in a mesh: lat: 8 (over z), lon: 128 (over x, y, core).
Axes of the slice: x: 8, y: 8, z: 8, core: 2. Of those that a mesh axis runs over, the one named last changes fastest.
Arguments:
- ensemble: bfloat16 [64, 2097152], P(None, ('lat', 'lon')), may hold values from -6 to 6
- leaf_basis: bfloat16 [16, 2097152], P(None, ('lat', 'lon')), may hold values from -0.75 to 0.75
- near_blocks: bfloat16 [32768, 64, 320], P(('lat', 'lon')), may hold values from -0.3125 to 0.3125
- local_transfer: float32 [1024, 64, 16, 16], P(('lat', 'lon')), may hold values from -1.5 to 1.5
- local_coupling: float32 [1024, 64, 16, 16], P(('lat', 'lon')), may hold values from -1 to 1
- upper_transfer: float32 [8, 256, 16, 16], P('lat'), may hold values from -1.5 to 1.5
- upper_coupling: float32 [8, 256, 16, 16], P('lat'), may hold values from -1 to 1
- pair_source: int32 [8, 128, 64], P('lat', 'lon'), may hold values from 0 to 95
- pair_target: int32 [8, 128, 64], P('lat', 'lon'), may hold values from 0 to 31
- pair_coupling: float32 [8, 128, 64, 16, 16], P('lat', 'lon'), may hold values from -1.5 to 1.5
Outputs:
- product_field: float32 [64, 2097152], P(None, ('lat', 'lon'))
The draws below stay inside these ranges and needn't reach their ends.
Inputs may be any that keep to these rules, and one draw needn't show every extreme that they name: `pair_source`: a pair's source names a leaf of the band below for values under 32, of the own band under 2 * 32, else of the band above.
All inputs are finite; a program needn't handle non-finite values.
Results may differ from the reference program's by a relative error of at most 0.0006.
Values may be sent and summed in bfloat16 or wider, within the bound.
A program may use at most 32 MiB of HBM per device.

```python
import jax
import jax.numpy as jnp
from jax import lax

R = 64
LEAF = 64
RANK = 16
SPAN = 2
LEAF_DEV = 32
PAIRS = 64
LEAVES = 32768
POINTS = 2097152
N_LAT = 8
N_LON = 128


def height_factors(node_count, top_height):
    factors = [2.0 ** (-0.5 * (top_height - max(int(node).bit_length() - 1, 0))) for node in range(node_count)]
    return jnp.asarray(factors, dtype=jnp.float32)


def coupling_values(key, shape):
    values = jax.random.normal(key, shape, jnp.float32)
    return jnp.clip(values, -4.0, 4.0) * float(RANK) ** (-0.5)


def draw_local_coupling(key, part):
    key = jax.random.fold_in(key, 11)
    top_height = LEAF_DEV.bit_length() - 1
    factors = height_factors(2 * LEAF_DEV, top_height)
    shape = (N_LAT * N_LON, 2 * LEAF_DEV, RANK, RANK)
    values = coupling_values(key, shape)
    return (values * factors[None, :, None, None]).astype(jnp.float32)


def draw_upper_coupling(key, part):
    key = jax.random.fold_in(key, 12)
    top_height = LEAF_DEV.bit_length() - 1 + (N_LON.bit_length() - 1)
    factors = height_factors(2 * N_LON, top_height)
    shape = (N_LAT, 2 * N_LON, RANK, RANK)
    values = coupling_values(key, shape)
    return (values * factors[None, :, None, None]).astype(jnp.float32)


def set_ends(values, own_key, smallest, high):
    longest = values.shape.index(max(values.shape))
    spots = []
    for shift in (0, 1):
        where = [jax.random.randint(jax.random.fold_in(own_key, axis), (), 0, length) for axis, length in enumerate(values.shape)]
        where[longest] = (where[longest] + shift) % values.shape[longest]
        spots.append(tuple(where))
    return values.at[spots[0]].set(smallest).at[spots[1]].set(high)


def levels(own_key, dims, pieces, smallest, high):
    def one(position, parts):
        heights = jax.random.uniform(jax.random.fold_in(jax.random.fold_in(own_key, 6), position), (parts,), jnp.float32, smallest / len(pieces), high / len(pieces))
        return jnp.repeat(jnp.exp(heights), dims[position] // parts).reshape((-1,) + (1,) * (len(dims) - position - 1))

    factor_of = one(*pieces[0])
    for cut in pieces[1:]:
        factor_of = factor_of * one(*cut)
    return factor_of


def bell_draw(stream_key, dims, deviation, reach, cuts=(), kind=jnp.bfloat16):
    array = jax.random.normal(stream_key, dims, jnp.float32) * deviation
    if len(cuts) > 0:
        array = levels(stream_key, dims, cuts, -0.22, 0.18) * array
    return jnp.clip(array, min=-reach, max=reach).astype(kind)


def setup_inputs(seed: int = 0) -> dict:
    splits = jax.random.split(jax.random.key(seed), 11)
    return {
        "ensemble": bell_draw(splits[0], (R, POINTS), 1.0, 6.0, ((1, 1024),)),
        "leaf_basis": bell_draw(splits[1], (RANK, POINTS), LEAF ** -0.5, 0.75, ((1, 1024),)),
        "near_blocks": bell_draw(splits[2], (LEAVES, LEAF, (2 * SPAN + 1) * LEAF), ((2 * SPAN + 1) * LEAF) ** -0.5, 0.3125, ((0, 1024),)),
        "local_transfer": bell_draw(splits[3], (N_LAT * N_LON, 2 * LEAF_DEV, RANK, RANK), RANK ** -0.5, 1.5, ((0, 1024),), jnp.float32),
        "local_coupling": draw_local_coupling(jax.random.fold_in(splits[10], 71), 0),
        "upper_transfer": bell_draw(splits[5], (N_LAT, 2 * N_LON, RANK, RANK), RANK ** -0.5, 1.5, ((0, 8),), jnp.float32),
        "upper_coupling": draw_upper_coupling(jax.random.fold_in(splits[10], 71), 0),
        "pair_source": set_ends(jax.random.randint(splits[7], (N_LAT, N_LON, PAIRS), 0, 3 * LEAF_DEV), jax.random.fold_in(splits[7], 1), 0, (3 * LEAF_DEV) - 1).astype(jnp.int32),
        "pair_target": set_ends(jax.random.randint(splits[8], (N_LAT, N_LON, PAIRS), 0, LEAF_DEV), jax.random.fold_in(splits[8], 1), 0, LEAF_DEV - 1).astype(jnp.int32),
        "pair_coupling": bell_draw(splits[9], (N_LAT, N_LON, PAIRS, RANK, RANK), RANK ** -0.5, 1.5, ((0, 8), (1, 128)), jnp.float32),
    }


def product(pattern, left_term, right_term):
    return jnp.einsum(pattern, left_term.astype(jnp.float32), right_term.astype(jnp.float32), precision=lax.Precision.HIGHEST)


def swapped_pairs(values):
    shaped = values.reshape(values.shape[:1] + (values.shape[1] // 2, 2) + values.shape[2:])
    return shaped[:, :, ::-1].reshape(values.shape)


def reference(ensemble, leaf_basis, near_blocks, local_transfer, local_coupling, upper_transfer, upper_coupling, pair_source, pair_target, pair_coupling):
    band_leaves = N_LON * LEAF_DEV
    leaf_total = N_LAT * band_leaves
    window_leaves = 2 * SPAN + 1
    leaves_x = ensemble.reshape(R, leaf_total, LEAF)
    leaves_u = leaf_basis.reshape(RANK, leaf_total, LEAF)
    leaf_sums = product("kgi,rgi->gkr", leaves_u, leaves_x)

    zero_leaves = jnp.zeros((R, SPAN, LEAF), ensemble.dtype)
    padded_x = jnp.concatenate([zero_leaves, leaves_x, zero_leaves], axis=1)
    blocks_by_band = near_blocks.reshape(N_LAT, band_leaves, LEAF, window_leaves * LEAF)

    def band_near(band_index):
        start_leaf = (band_index * band_leaves).astype(jnp.int32)
        window_x = lax.dynamic_slice_in_dim(padded_x, start_leaf, band_leaves + 2 * SPAN, 1)
        stacked = jnp.concatenate([window_x[:, offset:offset + band_leaves] for offset in range(window_leaves)], axis=2)
        blocks = lax.dynamic_index_in_dim(blocks_by_band, band_index, 0, keepdims=False)
        return product("gik,rgk->rgi", blocks, stacked)

    near_bands = lax.map(band_near, jnp.arange(N_LAT, dtype=jnp.int32))
    near_part = jnp.moveaxis(near_bands, 0, 1).reshape(R, leaf_total, LEAF)

    local_edges = local_transfer.reshape(N_LAT, N_LON, 2 * LEAF_DEV, RANK, RANK)
    local_links = local_coupling.reshape(N_LAT, N_LON, 2 * LEAF_DEV, RANK, RANK)
    tiers = []
    level_width = LEAF_DEV
    while level_width > 1:
        tiers.append((local_edges[:, :, level_width:2 * level_width].reshape(N_LAT, N_LON * level_width, RANK, RANK),
                      local_links[:, :, level_width:2 * level_width].reshape(N_LAT, N_LON * level_width, RANK, RANK)))
        level_width = level_width // 2
    level_width = N_LON
    while level_width > 1:
        tiers.append((upper_transfer[:, level_width:2 * level_width], upper_coupling[:, level_width:2 * level_width]))
        level_width = level_width // 2

    current = leaf_sums.reshape(N_LAT, band_leaves, RANK, R)
    climbed = []
    for edges, links in tiers:
        climbed.append(current)
        pushed = product("lnab,lnar->lnbr", edges, current)
        current = pushed[:, 0::2] + pushed[:, 1::2]

    downward = jnp.zeros((N_LAT, 1, RANK, R), jnp.float32)
    for tier_pair, below in reversed(list(zip(tiers, climbed))):
        edges, links = tier_pair
        parents = jnp.repeat(downward, 2, axis=1)
        downward = product("lnab,lnbr->lnar", edges, parents) + product("lnab,lnbr->lnar", links, swapped_pairs(below))

    band_sums = leaf_sums.reshape(N_LAT, N_LON, LEAF_DEV, RANK, R)
    zero_band = jnp.zeros((1, N_LON, LEAF_DEV, RANK, R), jnp.float32)
    padded_sums = jnp.concatenate([zero_band, band_sums, zero_band], axis=0)
    extended = jnp.concatenate([padded_sums[:-2], padded_sums[1:-1], padded_sums[2:]], axis=2)
    picked = jnp.take_along_axis(extended, pair_source[:, :, :, None, None], axis=2)
    coupled = product("lmpab,lmpbr->lmpar", pair_coupling, picked)
    targets = (pair_target[:, :, :, None] == jnp.arange(LEAF_DEV, dtype=jnp.int32)).astype(jnp.float32)
    added = product("lmpg,lmpar->lmgar", targets, coupled)
    leaf_down = downward.reshape(N_LAT, N_LON, LEAF_DEV, RANK, R) + added

    far_part = product("kgi,gkr->rgi", leaves_u, leaf_down.reshape(leaf_total, RANK, R))
    return (near_part + far_part).reshape(R, POINTS)
```

```python
import functools

import jax
import jax.numpy as jnp
from jax import lax
from jax.experimental import pallas as pl
from jax.experimental.pallas import tpu as pltpu
from jax.sharding import PartitionSpec as P

F32 = jnp.float32
BF16 = jnp.bfloat16
RANK = 16
LANES = 128
NODES = 8
MESH = pl.DeviceIdType.MESH


def iota(shape, axis):
    return lax.broadcasted_iota(jnp.int32, shape, axis)


def one_hot(mask):
    return jnp.where(mask, 1.0, 0.0).astype(BF16)


def nn(a, b):
    return lax.dot_general(a, b, (((1,), (0,)), ((), ())), preferred_element_type=F32)


def nt(a, b):
    return lax.dot_general(a, b, (((1,), (1,)), ((), ())), preferred_element_type=F32)


def split(x):
    high = x.astype(BF16)
    return high, (x - high.astype(F32)).astype(BF16)


def three(dot, a, b):
    return dot(a[0], b[0]) + (dot(a[0], b[1]) + dot(a[1], b[0]))


def picked_by(dot, a, b):
    return dot(a[0], b) + dot(a[1], b)


def picks(dot, a, b):
    return dot(a, b[0]) + dot(a, b[1])


def side_by_side(parts):
    return jnp.concatenate(parts, axis=1)


def rows_of(refs, first, count):
    return tuple(ref[pl.ds(first * LANES, count * LANES), :] for ref in refs)


def climb(leaves, count, edge):
    ups = {}
    if count < NODES:
        ups[0] = leaves[0]
    else:
        level = count // NODES
        for i, block in enumerate(leaves):
            ups[level + i] = block
        while level > 1:
            for i in range(level // 2, level):
                pair = side_by_side([ups[2 * i], ups[2 * i + 1]])
                ups[i] = three(nn, split(pair), edge(2 * i, 2))
            level //= 2
        ups[0] = three(nn, split(ups[1]), edge(1, 1))
    if count >= 4:
        ups[0] = ups[0] + three(nn, split(ups[0]), edge(0, 1))
    return ups


def descend(ups, count, edge, link):
    rows = ups[0].shape[0]
    top = three(nt, split(ups[0]), link(0, 1))
    if count >= 4:
        slot = iota((rows, LANES), 1) % NODES
        first = jnp.where((slot == 2) | (slot == 3), top, 0.0)
        top = top + three(nt, split(first), edge(0, 1))
    if count < NODES:
        return [top]
    level = [three(nt, split(ups[1]), link(1, 1)) + three(nt, split(top), edge(1, 1))]
    while len(level) < count // NODES:
        width = len(level)
        below = []
        for i, block in enumerate(level):
            node = width + i
            both = three(nt, split(block), edge(2 * node, 2))
            for side in range(2):
                child = 2 * node + side
                own = three(nt, split(ups[child]), link(child, 1))
                below.append(own + both[:, side * LANES : (side + 1) * LANES])
        level = below
    return level


def paths(count, edge):
    levels = []
    start = one_hot(iota((RANK, LANES), 1) == iota((RANK, LANES), 0) * NODES + 1)
    step = picks(nt, start, edge(0, 1))
    if count >= 4:
        step = three(nt, split(step), edge(0, 1))
    if count < NODES:
        return [[step]]
    levels.append([three(nt, split(step), edge(1, 1))])
    while len(levels[-1]) < count // NODES:
        width = len(levels[-1])
        below = []
        for i, block in enumerate(levels[-1]):
            both = three(nt, split(block), edge(2 * (width + i), 2))
            below += [both[:, :LANES], both[:, LANES:]]
        levels.append(below)
    return levels


def stacked(blocks):
    count = blocks
    members = min(count, NODES)
    offset = count if count < NODES else 0
    row = iota((members * RANK, LANES), 0)
    lane = iota((members * RANK, LANES), 1)
    return one_hot(lane == (row % RANK) * NODES + row // RANK + offset)


def operators(turned, masks, edge_refs, block, spread):
    (high, low), mask = turned, masks
    nodes = high.shape[0]
    for half in range(2):
        cut = slice(half * LANES, (half + 1) * LANES)
        both = jnp.concatenate([high[:, cut], low[:, cut]], axis=0)
        for pair in range(NODES // 2):
            wide = nn(both, spread[pair])
            parts = [
                [
                    jnp.where(mask, wide[k * nodes : (k + 1) * nodes, s * LANES : (s + 1) * LANES], 0.0)
                    for s in range(2)
                ]
                for k in range(2)
            ]
            for k in range(2):
                for j in range(nodes // NODES):
                    rows = slice(j * NODES, (j + 1) * NODES)
                    tile = jnp.concatenate([parts[k][0][rows], parts[k][1][rows]], axis=0)
                    start = (block + j) * LANES + (half * NODES + 2 * pair) * NODES
                    edge_refs[k][start : start + 2 * NODES, :] = tile.astype(BF16)


def kernel(
    sizes,
    ensemble,
    basis,
    near,
    local_edge,
    local_link,
    upper_edge,
    upper_link,
    source,
    target,
    pair_link,
    out_ref,
    x_ref,
    basis_ref,
    near_ref,
    le_ref,
    ll_ref,
    ue_ref,
    ul_ref,
    src_ref,
    tgt_ref,
    pl_ref,
    eh_ref,
    el_ref,
    vh_ref,
    vl_ref,
    basis_blocks,
    ext_ref,
    members_ref,
    groups_ref,
    final_ref,
    load_sem,
    send_sem,
    member_sem,
    group_sem,
    side_sem,
):
    n_lat, groups, members = sizes
    n_lon = groups * members
    vectors, points = ensemble.shape
    leaves = near.shape[0]
    leaf_points = near.shape[1]
    halo = near.shape[2] // 2 - leaf_points // 2
    lat, lon = lax.axis_index("lat"), lax.axis_index("lon")
    group, member = lon // members, lon % members
    flat = lat * n_lon + lon
    total = n_lat * n_lon

    def at(index):
        index = lax.rem(index, total)
        return (index // n_lon, lax.rem(index, n_lon))

    member_peers = [(lat, group * members + lax.rem(member + j, members)) for j in range(1, members)]
    group_peers = [(lat, lax.rem(group + j, groups) * members + member) for j in range(1, groups)]
    above = (lax.rem(lat + 1, n_lat), lon)
    below = (lax.rem(lat + n_lat - 1, n_lat), lon)
    after, before = at(flat + 1), at(flat + total - 1)

    own_points = x_ref.at[:, halo : halo + points]
    loads = [
        pltpu.make_async_copy(src, dst, load_sem.at[i])
        for i, (src, dst) in enumerate(
            [
                (local_edge, le_ref),
                (basis, basis_ref),
                (ensemble, own_points),
                (local_link, ll_ref),
                (upper_edge, ue_ref),
                (upper_link, ul_ref),
                (source, src_ref),
                (target, tgt_ref),
                (pair_link, pl_ref),
                (near, near_ref),
            ]
        )
    ]
    for load in loads:
        load.start()

    barrier = pltpu.get_barrier_semaphore()
    peers = member_peers + group_peers + [above, below, after, before]
    for peer in peers:
        pl.semaphore_signal(barrier, inc=1, device_id=peer, device_id_type=MESH)

    row, lane = iota((LANES, LANES), 0), iota((LANES, LANES), 1)
    offset = row - lane // NODES
    spread = []
    for pair in range(NODES // 2):
        spread.append(
            side_by_side([one_hot(offset == (2 * pair + s) * RANK) for s in range(2)])
        )

    def masks(count, slots):
        node_slot = slots(iota((count, LANES), 0))
        column = iota((count, LANES), 1) % NODES
        inner = node_slot >= 2
        edge = inner & (column == (node_slot // 2) % NODES)
        link = inner & (column == (node_slot + 1 - 2 * (node_slot % 2)) % NODES)
        return edge, link

    eye = one_hot(iota((2 * leaves, 2 * leaves), 0) == iota((2 * leaves, 2 * leaves), 1))
    local_masks = masks(2 * leaves, lambda r: r)

    def turned(ref, chosen):
        parts = split(ref[...])
        return tuple(nt(chosen, part).astype(BF16) for part in parts)

    edges, links = (eh_ref, el_ref), (vh_ref, vl_ref)
    local_blocks = 2 * leaves // NODES
    member_blocks = max(1, 2 * members // NODES)
    group_blocks = max(1, 2 * groups // NODES)

    def reader(refs, base):
        return lambda first, count: rows_of(refs, base + first, count)

    local_e, local_v = reader(edges, 0), reader(links, 0)
    member_e, member_v = reader(edges, local_blocks), reader(links, local_blocks)
    group_base = local_blocks + member_blocks
    group_e, group_v = reader(edges, group_base), reader(links, group_base)

    loads[0].wait()
    operators(turned(le_ref, eye), local_masks[0], edges, 0, spread)

    loads[1].wait()
    width = NODES * leaf_points
    leaf_blocks = leaves // NODES
    keep = iota((NODES, width), 0) == iota((NODES, width), 1) // leaf_points
    for j in range(leaf_blocks):
        part = basis_ref[:, j * width : (j + 1) * width].astype(F32)
        for k in range(0, RANK, 2):
            tiles = [
                jnp.where(keep, jnp.broadcast_to(part[k + s : k + s + 1], (NODES, width)), 0.0)
                for s in range(2)
            ]
            basis_blocks[j, k * NODES : (k + 2) * NODES, :] = jnp.concatenate(tiles, axis=0).astype(BF16)
    loads[2].wait()
    sums_across = []
    for j in range(leaf_blocks):
        x_part = x_ref[:, halo + j * width : halo + (j + 1) * width]
        sums_across.append(nt(x_part, basis_blocks[j]))
        by_rank = nt(basis_blocks[j], x_part)
        for k in range(RANK // 2):
            ext_ref[leaves + j * NODES : leaves + (j + 1) * NODES, k * LANES : (k + 1) * LANES] = side_by_side(
                [
                    by_rank[k * NODES : (k + 1) * NODES],
                    by_rank[(k + RANK // 2) * NODES : (k + RANK // 2 + 1) * NODES],
                ]
            )

    local_ups = climb(sums_across, leaves, local_e)
    local_paths = paths(leaves, local_e)
    device_sum = three(nt, split(local_paths[0][0]), split(local_ups[1]))
    empty = jnp.zeros((RANK, LANES - vectors), F32)
    own_member = members_ref.at[pl.ds(member * RANK, RANK)]
    own_member[...] = side_by_side([device_sum, empty])

    pl.semaphore_wait(barrier, len(peers))

    def send(src, dst, index, arrived, peer):
        copy = pltpu.make_async_remote_copy(
            src_ref=src,
            dst_ref=dst,
            send_sem=send_sem.at[index],
            recv_sem=arrived,
            device_id=peer,
            device_id_type=MESH,
        )
        copy.start()
        return copy

    member_copies = [
        send(own_member, own_member, j, member_sem.at[j], peer) for j, peer in enumerate(member_peers)
    ]
    used = len(member_peers)
    own_sums = ext_ref.at[leaves : 2 * leaves]
    side_copies = [
        send(x_ref.at[:, points : points + halo], x_ref.at[:, 0:halo], used, side_sem.at[0], after),
        send(
            x_ref.at[:, halo : 2 * halo],
            x_ref.at[:, halo + points : points + 2 * halo],
            used + 1,
            side_sem.at[1],
            before,
        ),
        send(own_sums, ext_ref.at[0:leaves], used + 2, side_sem.at[2], above),
        send(own_sums, ext_ref.at[2 * leaves : 3 * leaves], used + 3, side_sem.at[3], below),
    ]
    used += 4

    member_slots, group_slots = member_blocks * NODES, group_blocks * NODES
    upper_rows = member_slots + group_slots
    upper_nodes = upper_edge.shape[1]
    slot = iota((upper_rows, upper_nodes), 0)
    scale = jnp.where(slot >= 2, 2, 1)
    for power in range(2, members.bit_length()):
        scale = jnp.where(slot >= 2**power, 2**power, scale)
    wanted = jnp.where(slot < member_slots, slot + (groups + group - 1) * scale, slot - member_slots)
    chosen = one_hot(wanted == iota((upper_rows, upper_nodes), 1))
    upper_masks = masks(upper_rows, lambda r: jnp.where(r < member_slots, r, r - member_slots))
    loads[4].wait()
    operators(turned(ue_ref, chosen), upper_masks[0], edges, local_blocks, spread)

    member_order = stacked(members)
    member_paths = paths(members, member_e)[-1]
    to_group = [split(picked_by(nt, split(block), member_order)) for block in member_paths]

    loads[3].wait()
    operators(turned(ll_ref, eye), local_masks[1], links, 0, spread)
    loads[5].wait()
    operators(turned(ul_ref, chosen), upper_masks[1], links, local_blocks, spread)

    for copy in member_copies:
        copy.wait_recv()
    member_sums = members_ref[...]
    member_parts = split(member_sums)
    per_block = min(members, NODES) * RANK
    group_sum = None
    for i, block in enumerate(to_group):
        cut = slice(i * per_block, (i + 1) * per_block)
        term = three(nn, block, (member_parts[0][cut], member_parts[1][cut]))
        group_sum = term if group_sum is None else group_sum + term
    own_group = groups_ref.at[pl.ds(group * RANK, RANK)]
    own_group[...] = group_sum

    group_copies = [
        send(own_group, own_group, used + j, group_sem.at[j], peer) for j, peer in enumerate(group_peers)
    ]

    repeat = iota((LANES, LANES), 1)
    rank_lane = jnp.where(repeat < 3 * RANK, repeat % RANK, -1)
    own_slots = []
    for i in range(len(member_paths)):
        mine = member - i * NODES if members >= NODES else member + members
        own_slots.append(one_hot((row // NODES == rank_lane) & (row % NODES == mine)))
    own_path = None
    for block, pick in zip(member_paths, own_slots):
        term = picked_by(nn, split(block), pick)
        own_path = term if own_path is None else own_path + term
    group_slot = group if groups >= NODES else group + groups
    lift = one_hot(
        (iota((LANES, RANK), 0) // NODES == iota((LANES, RANK), 1))
        & (iota((LANES, RANK), 0) % NODES == group_slot)
    )
    lifted = split(picks(nn, lift, split(own_path)))
    group_ups = climb([stacked(groups).astype(F32)], groups, group_e)
    group_map = descend(group_ups, groups, group_e, group_v)[0]
    group_map = split(three(nn, split(group_map), lifted))

    member_across = []
    turned_sums = jnp.transpose(member_sums)[:vectors]
    for i in range(len(member_paths)):
        part = split(turned_sums[:, i * per_block : (i + 1) * per_block])
        member_across.append(picked_by(nn, part, member_order))
    member_ups = climb(member_across, members, member_e)
    down_here = None
    for block, pick in zip(descend(member_ups, members, member_e, member_v), own_slots):
        term = picked_by(nn, split(block), pick)
        down_here = term if down_here is None else down_here + term

    for j in range(leaf_blocks):
        folded = split(picked_by(nn, split(local_paths[-1][j]), basis_blocks[j]))
        cut = slice(j * width, (j + 1) * width)
        final_ref[0:RANK, cut] = folded[0]
        final_ref[RANK : 2 * RANK, cut] = folded[0]
        final_ref[2 * RANK : 3 * RANK, cut] = folded[1]

    local_down = descend(local_ups, leaves, local_e, local_v)

    loads[9].wait()
    side_copies[0].wait_recv()
    side_copies[1].wait_recv()

    @pl.when(flat == 0)
    def _():
        x_ref[:, 0:halo] = jnp.zeros((vectors, halo), BF16)

    @pl.when(flat == total - 1)
    def _():
        x_ref[:, halo + points :] = jnp.zeros((vectors, halo), BF16)

    blank = jnp.zeros((leaf_points, leaf_points), BF16)
    pair_points = 2 * leaf_points
    span = near.shape[2] + leaf_points
    for j in range(leaves // 2):
        first = side_by_side([near_ref[2 * j], blank])
        second = side_by_side([blank, near_ref[2 * j + 1]])
        weights = jnp.concatenate([first, second], axis=0)
        window = x_ref[:, j * pair_points : j * pair_points + span]
        out_ref[:, j * pair_points : (j + 1) * pair_points] = nt(window, weights)

    for load in loads[6:9]:
        load.wait()
    side_copies[2].wait_recv()
    side_copies[3].wait_recv()
    pairs = source.shape[1]
    spot = iota((3 * leaves, pairs), 0)
    inside = ((spot >= leaves) | (lat > 0)) & ((spot < 2 * leaves) | (lat < n_lat - 1))
    reads = jnp.where((spot == src_ref[...]) & inside, 1.0, 0.0)
    reads = jnp.transpose(reads).astype(BF16)
    found = [nn(reads, part) for part in split(ext_ref[...])]
    half = RANK // 2
    wide_target = side_by_side([tgt_ref[...], tgt_ref[...]])
    hits = jnp.where(iota((leaves, 2 * pairs), 0) == wide_target, 1.0, 0.0)
    link_rows = pl_ref[...].reshape(RANK, 2, half, pairs)
    link_rows = jnp.concatenate([link_rows[:, 0], link_rows[:, 1]], axis=2)
    link_high = link_rows.astype(BF16).astype(F32)
    link_parts = (link_high, link_rows - link_high)
    rights = [[], []]
    for k in range(half):
        for s in range(2):
            tile = found[s][:, k * LANES : (k + 1) * LANES]
            rights[s].append(jnp.concatenate([tile[:, :vectors], tile[:, vectors:]], axis=0))
    rights = [jnp.concatenate(r, axis=0).astype(BF16) for r in rights]
    for j in range(leaf_blocks):
        hit = hits[j * NODES : (j + 1) * NODES]
        lefts = []
        for part in link_parts:
            columns = []
            for k in range(half):
                columns.append(
                    jnp.concatenate([hit * part[a, k : k + 1] for a in range(RANK)], axis=0).astype(BF16)
                )
            lefts.append(side_by_side(columns))
        added = three(nn, lefts, rights)
        down = local_down[j] + jnp.transpose(added)
        cut = slice(j * width, (j + 1) * width)
        out_ref[:, cut] = out_ref[:, cut] + picked_by(nn, split(down), basis_blocks[j])

    for copy in group_copies:
        copy.wait_recv()
    other_sums = jnp.transpose(groups_ref[...])[:vectors]
    down_here = down_here + three(nn, split(other_sums), group_map)
    down_parts = split(down_here)
    lanes3 = iota((vectors, LANES), 1)
    middle = (lanes3 >= RANK) & (lanes3 < 2 * RANK)
    down3 = jnp.where(middle, down_parts[1].astype(F32), down_parts[0].astype(F32))
    down3 = down3[:, : 3 * RANK].astype(BF16)
    for j in range(leaf_blocks):
        cut = slice(j * width, (j + 1) * width)
        out_ref[:, cut] = out_ref[:, cut] + nn(down3, final_ref[:, cut])

    for copy in member_copies + side_copies + group_copies:
        copy.wait_send()


def split_lon(n_lon):
    members = 16 if n_lon >= 128 else 1 << n_lon.bit_length() // 2
    return n_lon // members, members


def shards(
    n_lat,
    n_lon,
    ensemble,
    leaf_basis,
    near_blocks,
    local_transfer,
    local_coupling,
    upper_transfer,
    upper_coupling,
    pair_source,
    pair_target,
    pair_coupling,
):
    vectors, points = ensemble.shape
    leaves, leaf_points, window = near_blocks.shape
    halo = window // 2 - leaf_points // 2
    groups, members = split_lon(n_lon)
    pairs = pair_source.shape[2]

    def by_node(matrices):
        nodes = matrices.shape[1]
        return jnp.transpose(matrices[0], (1, 2, 0)).reshape(RANK * RANK, nodes)

    member_blocks = max(1, 2 * members // NODES)
    group_blocks = max(1, 2 * groups // NODES)
    blocks = 2 * leaves // NODES + member_blocks + group_blocks
    upper_nodes = upper_transfer.shape[1]
    operands = (
        ensemble,
        leaf_basis,
        near_blocks,
        by_node(local_transfer),
        by_node(local_coupling),
        by_node(upper_transfer),
        by_node(upper_coupling),
        pair_source[0],
        pair_target[0],
        by_node(pair_coupling[0]),
    )
    return pl.pallas_call(
        functools.partial(kernel, (n_lat, groups, members)),
        out_shape=jax.ShapeDtypeStruct((vectors, points), F32),
        in_specs=[pl.BlockSpec(memory_space=pl.ANY)] * len(operands),
        out_specs=pl.BlockSpec(memory_space=pltpu.VMEM),
        scratch_shapes=[
            pltpu.VMEM((vectors, points + 2 * halo), BF16),
            pltpu.VMEM((RANK, points), BF16),
            pltpu.VMEM(near_blocks.shape, BF16),
            pltpu.VMEM((RANK * RANK, 2 * leaves), F32),
            pltpu.VMEM((RANK * RANK, 2 * leaves), F32),
            pltpu.VMEM((RANK * RANK, upper_nodes), F32),
            pltpu.VMEM((RANK * RANK, upper_nodes), F32),
            pltpu.VMEM((1, pairs), jnp.int32),
            pltpu.VMEM((1, pairs), jnp.int32),
            pltpu.VMEM((RANK * RANK, pairs), F32),
            pltpu.VMEM((blocks * LANES, LANES), BF16),
            pltpu.VMEM((blocks * LANES, LANES), BF16),
            pltpu.VMEM((blocks * LANES, LANES), BF16),
            pltpu.VMEM((blocks * LANES, LANES), BF16),
            pltpu.VMEM((leaves // NODES, LANES, NODES * leaf_points), BF16),
            pltpu.VMEM((3 * leaves, RANK * vectors), F32),
            pltpu.VMEM((members * RANK, LANES), F32),
            pltpu.VMEM((groups * RANK, LANES), F32),
            pltpu.VMEM((3 * RANK, points), BF16),
            pltpu.SemaphoreType.DMA((len(operands),)),
            pltpu.SemaphoreType.DMA((members + groups + 2,)),
            pltpu.SemaphoreType.DMA((members - 1,)),
            pltpu.SemaphoreType.DMA((groups - 1,)),
            pltpu.SemaphoreType.DMA((4,)),
        ],
        compiler_params=pltpu.CompilerParams(
            collective_id=0, has_side_effects=True, vmem_limit_bytes=60 * 2**20
        ),
        name="h2_matvec",
    )(*operands)


def solution(mesh):
    return jax.shard_map(
        functools.partial(shards, mesh.shape["lat"], mesh.shape["lon"]),
        mesh=mesh,
        in_specs=(
            P(None, ("lat", "lon")),
            P(None, ("lat", "lon")),
            P(("lat", "lon"), None, None),
            P(("lat", "lon"), None, None, None),
            P(("lat", "lon"), None, None, None),
            P("lat", None, None, None),
            P("lat", None, None, None),
            P("lat", "lon", None),
            P("lat", "lon", None),
            P("lat", "lon", None, None, None),
        ),
        out_specs=P(None, ("lat", "lon")),
        check_vma=False,
    )
```

```python
import functools

import jax
import jax.numpy as jnp
from jax import lax
from jax.experimental import pallas as pl
from jax.experimental.pallas import tpu as pltpu
from jax.sharding import PartitionSpec as P

F32 = jnp.float32
BF16 = jnp.bfloat16
RANK = 16
LANES = 128
NODES = 8
MESH = pl.DeviceIdType.MESH


def iota(shape, axis):
    return lax.broadcasted_iota(jnp.int32, shape, axis)


def one_hot(mask):
    return jnp.where(mask, 1.0, 0.0).astype(BF16)


def nn(a, b):
    return lax.dot_general(a, b, (((1,), (0,)), ((), ())), preferred_element_type=F32)


def nt(a, b):
    return lax.dot_general(a, b, (((1,), (1,)), ((), ())), preferred_element_type=F32)


def split(x):
    high = x.astype(BF16)
    return high, (x - high.astype(F32)).astype(BF16)


def three(dot, a, b):
    return dot(a[0], b[0]) + (dot(a[0], b[1]) + dot(a[1], b[0]))


def picked_by(dot, a, b):
    return dot(a[0], b) + dot(a[1], b)


def picks(dot, a, b):
    return dot(a, b[0]) + dot(a, b[1])


def side_by_side(parts):
    return jnp.concatenate(parts, axis=1)


def rows_of(refs, first, count):
    return tuple(ref[pl.ds(first * LANES, count * LANES), :] for ref in refs)


def climb(leaves, count, edge):
    ups = {}
    if count < NODES:
        ups[0] = leaves[0]
    else:
        level = count // NODES
        for i, block in enumerate(leaves):
            ups[level + i] = block
        while level > 1:
            for i in range(level // 2, level):
                pair = side_by_side([ups[2 * i], ups[2 * i + 1]])
                ups[i] = three(nn, split(pair), edge(2 * i, 2))
            level //= 2
        ups[0] = three(nn, split(ups[1]), edge(1, 1))
    if count >= 4:
        ups[0] = ups[0] + three(nn, split(ups[0]), edge(0, 1))
    return ups


def descend(ups, count, edge, link):
    rows = ups[0].shape[0]
    top = three(nt, split(ups[0]), link(0, 1))
    if count >= 4:
        slot = iota((rows, LANES), 1) % NODES
        first = jnp.where((slot == 2) | (slot == 3), top, 0.0)
        top = top + three(nt, split(first), edge(0, 1))
    if count < NODES:
        return [top]
    level = [three(nt, split(ups[1]), link(1, 1)) + three(nt, split(top), edge(1, 1))]
    while len(level) < count // NODES:
        width = len(level)
        below = []
        for i, block in enumerate(level):
            node = width + i
            both = three(nt, split(block), edge(2 * node, 2))
            for side in range(2):
                child = 2 * node + side
                own = three(nt, split(ups[child]), link(child, 1))
                below.append(own + both[:, side * LANES : (side + 1) * LANES])
        level = below
    return level


def paths(count, edge):
    levels = []
    start = one_hot(iota((RANK, LANES), 1) == iota((RANK, LANES), 0) * NODES + 1)
    step = picks(nt, start, edge(0, 1))
    if count >= 4:
        step = three(nt, split(step), edge(0, 1))
    if count < NODES:
        return [[step]]
    levels.append([three(nt, split(step), edge(1, 1))])
    while len(levels[-1]) < count // NODES:
        width = len(levels[-1])
        below = []
        for i, block in enumerate(levels[-1]):
            both = three(nt, split(block), edge(2 * (width + i), 2))
            below += [both[:, :LANES], both[:, LANES:]]
        levels.append(below)
    return levels


def stacked(blocks):
    count = blocks
    members = min(count, NODES)
    offset = count if count < NODES else 0
    row = iota((members * RANK, LANES), 0)
    lane = iota((members * RANK, LANES), 1)
    return one_hot(lane == (row % RANK) * NODES + row // RANK + offset)


def operators(turned, masks, edge_refs, block, spread):
    (high, low), mask = turned, masks
    nodes = high.shape[0]
    for half in range(2):
        cut = slice(half * LANES, (half + 1) * LANES)
        both = jnp.concatenate([high[:, cut], low[:, cut]], axis=0)
        for pair in range(NODES // 2):
            wide = nn(both, spread[pair])
            parts = [
                [
                    jnp.where(mask, wide[k * nodes : (k + 1) * nodes, s * LANES : (s + 1) * LANES], 0.0)
                    for s in range(2)
                ]
                for k in range(2)
            ]
            for k in range(2):
                for j in range(nodes // NODES):
                    rows = slice(j * NODES, (j + 1) * NODES)
                    tile = jnp.concatenate([parts[k][0][rows], parts[k][1][rows]], axis=0)
                    start = (block + j) * LANES + (half * NODES + 2 * pair) * NODES
                    edge_refs[k][start : start + 2 * NODES, :] = tile.astype(BF16)


def kernel(
    sizes,
    ensemble,
    basis,
    near,
    local_edge,
    local_link,
    upper_edge,
    upper_link,
    source,
    target,
    pair_link,
    acc_ref,
    final_ref,
    down_ref,
    x_ref,
    basis_ref,
    near_ref,
    le_ref,
    ll_ref,
    ue_ref,
    ul_ref,
    src_ref,
    tgt_ref,
    pl_ref,
    eh_ref,
    el_ref,
    vh_ref,
    vl_ref,
    basis_blocks,
    across_ref,
    ext_ref,
    members_ref,
    groups_ref,
    to_group_ref,
    map_ref,
    local_down_ref,
    pair_high_ref,
    pair_low_ref,
    load_sem,
    send_sem,
    member_sem,
    group_sem,
    side_sem,
):
    n_lat, groups, members = sizes
    n_lon = groups * members
    vectors, points = ensemble.shape
    leaves = near.shape[0]
    leaf_points = near.shape[1]
    halo = near.shape[2] // 2 - leaf_points // 2
    lat, lon = lax.axis_index("lat"), lax.axis_index("lon")
    group, member = lon // members, lax.rem(lon, members)
    flat = lat * n_lon + lon
    total = n_lat * n_lon

    member_peers = [(lat, group * members + lax.rem(member + j, members)) for j in range(1, members)]
    group_peers = [(lat, lax.rem(group + j, groups) * members + member) for j in range(1, groups)]
    after, before = flat < total - 1, flat > 0
    above, below = lat < n_lat - 1, lat > 0
    sides = [
        (after, ((flat + 1) // n_lon, lax.rem(flat + 1, n_lon))),
        (before, ((flat - 1) // n_lon, lax.rem(flat + total - 1, n_lon))),
        (above, (lat + 1, lon)),
        (below, (lat - 1, lon)),
    ]

    own_points = x_ref.at[:, halo : halo + points]
    loads = [
        pltpu.make_async_copy(src, dst, load_sem.at[i])
        for i, (src, dst) in enumerate(
            [
                (local_edge, le_ref),
                (basis, basis_ref),
                (ensemble, own_points),
                (local_link, ll_ref),
                (upper_edge, ue_ref),
                (upper_link, ul_ref),
                (source, src_ref),
                (target, tgt_ref),
                (pair_link, pl_ref),
                (near, near_ref),
            ]
        )
    ]
    for load in loads:
        load.start()

    barrier = pltpu.get_barrier_semaphore()
    for peer in member_peers + group_peers:
        pl.semaphore_signal(barrier, inc=1, device_id=peer, device_id_type=MESH)
    for there, peer in sides:

        @pl.when(there)
        def _():
            pl.semaphore_signal(barrier, inc=1, device_id=peer, device_id_type=MESH)

    row, lane = iota((LANES, LANES), 0), iota((LANES, LANES), 1)
    offset = row - lane // NODES
    spread = []
    for pair in range(NODES // 2):
        spread.append(
            side_by_side([one_hot(offset == (2 * pair + s) * RANK) for s in range(2)])
        )

    def masks(count, slots):
        node_slot = slots(iota((count, LANES), 0))
        column = iota((count, LANES), 1) % NODES
        inner = node_slot >= 2
        edge = inner & (column == (node_slot // 2) % NODES)
        link = inner & (column == (node_slot + 1 - 2 * (node_slot % 2)) % NODES)
        return edge, link

    eye = one_hot(iota((2 * leaves, 2 * leaves), 0) == iota((2 * leaves, 2 * leaves), 1))
    local_masks = masks(2 * leaves, lambda r: r)

    def turned(ref, chosen):
        parts = split(ref[...])
        return tuple(nt(chosen, part).astype(BF16) for part in parts)

    edges, links = (eh_ref, el_ref), (vh_ref, vl_ref)
    local_blocks = 2 * leaves // NODES
    member_blocks = max(1, 2 * members // NODES)
    group_blocks = max(1, 2 * groups // NODES)

    def reader(refs, base):
        return lambda first, count: rows_of(refs, base + first, count)

    local_e, local_v = reader(edges, 0), reader(links, 0)
    member_e, member_v = reader(edges, local_blocks), reader(links, local_blocks)
    group_base = local_blocks + member_blocks
    group_e, group_v = reader(edges, group_base), reader(links, group_base)

    for load in loads[:3]:
        load.wait()
    operators(turned(le_ref, eye), local_masks[0], edges, 0, spread)
    width = NODES * leaf_points
    leaf_blocks = leaves // NODES
    keep = iota((NODES, width), 0) == iota((NODES, width), 1) // leaf_points
    for j in range(leaf_blocks):
        part = basis_ref[:, j * width : (j + 1) * width].astype(F32)
        for k in range(0, RANK, 2):
            tiles = [
                jnp.where(keep, jnp.broadcast_to(part[k + s : k + s + 1], (NODES, width)), 0.0)
                for s in range(2)
            ]
            basis_blocks[j, k * NODES : (k + 2) * NODES, :] = jnp.concatenate(tiles, axis=0).astype(BF16)
    across = []
    for j in range(leaf_blocks):
        x_part = x_ref[:, halo + j * width : halo + (j + 1) * width]
        across.append(nt(x_part, basis_blocks[j]))
        across_ref[:, j * LANES : (j + 1) * LANES] = across[j]
    start = one_hot(iota((RANK, LANES), 1) == iota((RANK, LANES), 0) * NODES + 1)
    top = picks(nt, start, local_e(0, 1))
    top = three(nt, split(top), local_e(0, 1))
    top = three(nt, split(top), local_e(1, 1))
    halves = [
        three(nn, split(side_by_side([across[2 * i], across[2 * i + 1]])), local_e(leaf_blocks + 2 * i, 2))
        for i in range(leaf_blocks // 2)
    ]
    eighth = three(nn, split(side_by_side(halves)), local_e(2, 2))
    device_sum = three(nt, split(top), split(eighth))
    empty = jnp.zeros((RANK, LANES - vectors), F32)
    own_member = members_ref.at[pl.ds(member * RANK, RANK)]
    own_member[...] = side_by_side([device_sum, empty])

    def copy_to(src, dst, index, arrived, peer):
        return pltpu.make_async_remote_copy(
            src_ref=src,
            dst_ref=dst,
            send_sem=send_sem.at[index],
            recv_sem=arrived,
            device_id=peer,
            device_id_type=MESH,
        )

    own_sums = ext_ref.at[leaves : 2 * leaves]
    first_halo, last_halo = x_ref.at[:, halo : 2 * halo], x_ref.at[:, points : points + halo]
    left_halo, right_halo = x_ref.at[:, 0:halo], x_ref.at[:, halo + points : points + 2 * halo]
    below_sums, above_sums = ext_ref.at[0:leaves], ext_ref.at[2 * leaves : 3 * leaves]
    member_copies = [
        copy_to(own_member, own_member, j, member_sem.at[j], peer) for j, peer in enumerate(member_peers)
    ]
    used = len(member_peers)
    side_copies = [
        copy_to(src, dst, used + i, side_sem.at[i], sides[i][1])
        for i, (src, dst) in enumerate(
            [
                (last_halo, left_halo),
                (first_halo, right_halo),
                (own_sums, below_sums),
                (own_sums, above_sums),
            ]
        )
    ]
    used += 4
    own_group = groups_ref.at[pl.ds(group * RANK, RANK)]
    group_copies = [
        copy_to(own_group, own_group, used + j, group_sem.at[j], peer) for j, peer in enumerate(group_peers)
    ]

    def exchange():
        count = len(member_peers) + len(group_peers)
        for there, _ in sides:
            count = count + jnp.where(there, 1, 0)
        pl.semaphore_wait(barrier, count)
        for copy in member_copies:
            copy.start()
        for (there, _), copy in zip(sides, side_copies):
            pl.when(there)(copy.start)

    for j in range(leaf_blocks):
        x_part = x_ref[:, halo + j * width : halo + (j + 1) * width]
        by_rank = nt(basis_blocks[j], x_part)
        for k in range(RANK // 2):
            ext_ref[leaves + j * NODES : leaves + (j + 1) * NODES, k * LANES : (k + 1) * LANES] = side_by_side(
                [
                    by_rank[k * NODES : (k + 1) * NODES],
                    by_rank[(k + RANK // 2) * NODES : (k + RANK // 2 + 1) * NODES],
                ]
            )

    soon = (lat > 0) | (lon == 0)
    pl.when(soon)(exchange)

    member_slots, group_slots = member_blocks * NODES, group_blocks * NODES
    upper_rows = member_slots + group_slots
    upper_nodes = upper_edge.shape[1]
    slot = iota((upper_rows, upper_nodes), 0)
    scale = jnp.where(slot >= 2, 2, 1)
    for power in range(2, members.bit_length()):
        scale = jnp.where(slot >= 2**power, 2**power, scale)
    wanted = jnp.where(slot < member_slots, slot + (groups + group - 1) * scale, slot - member_slots)
    chosen = one_hot(wanted == iota((upper_rows, upper_nodes), 1))
    upper_masks = masks(upper_rows, lambda r: jnp.where(r < member_slots, r, r - member_slots))
    for load in loads[3:]:
        load.wait()
    operators(turned(ue_ref, chosen), upper_masks[0], edges, local_blocks, spread)
    operators(turned(ul_ref, chosen), upper_masks[1], links, local_blocks, spread)
    operators(turned(ll_ref, eye), local_masks[1], links, 0, spread)

    per_block = min(members, NODES) * RANK
    member_order = stacked(members)
    member_paths = paths(members, member_e)[-1]
    for i, block in enumerate(member_paths):
        cut = slice(i * per_block, (i + 1) * per_block)
        high, low = split(picked_by(nt, split(block), member_order))
        to_group_ref[0:RANK, cut] = high
        to_group_ref[RANK : 2 * RANK, cut] = low

    repeat = iota((LANES, LANES), 1)
    rank_lane = jnp.where(repeat < 3 * RANK, repeat % RANK, -1)

    def own_slots():
        picks_own = []
        for i in range(len(member_paths)):
            mine = member - i * NODES if members >= NODES else member + members
            picks_own.append(one_hot((row // NODES == rank_lane) & (row % NODES == mine)))
        return picks_own

    own_path = None
    for block, pick in zip(member_paths, own_slots()):
        term = picked_by(nn, split(block), pick)
        own_path = term if own_path is None else own_path + term
    group_slot = group if groups >= NODES else group + groups
    lift = one_hot(
        (iota((LANES, RANK), 0) // NODES == iota((LANES, RANK), 1))
        & (iota((LANES, RANK), 0) % NODES == group_slot)
    )
    lifted = split(picks(nn, lift, split(own_path)))
    group_ups = climb([stacked(groups).astype(F32)], groups, group_e)
    group_map = split(three(nn, split(descend(group_ups, groups, group_e, group_v)[0]), lifted))
    map_ref[0] = group_map[0]
    map_ref[1] = group_map[1]

    local_ups = climb([across_ref[:, j * LANES : (j + 1) * LANES] for j in range(leaf_blocks)], leaves, local_e)
    for j, block in enumerate(descend(local_ups, leaves, local_e, local_v)):
        local_down_ref[:, j * LANES : (j + 1) * LANES] = block
    for j, block in enumerate(paths(leaves, local_e)[-1]):
        folded = split(picked_by(nn, split(block), basis_blocks[j]))
        cut = slice(j * width, (j + 1) * width)
        final_ref[0:RANK, cut] = folded[0]
        final_ref[RANK : 2 * RANK, cut] = folded[0]
        final_ref[2 * RANK : 3 * RANK, cut] = folded[1]

    blank = jnp.zeros((leaf_points, leaf_points), BF16)
    pair_points = 2 * leaf_points
    span = near.shape[2] + leaf_points

    def near_part(j):
        first = side_by_side([near_ref[2 * j], blank])
        second = side_by_side([blank, near_ref[2 * j + 1]])
        weights = jnp.concatenate([first, second], axis=0)
        window = x_ref[:, j * pair_points : j * pair_points + span]
        acc_ref[:, j * pair_points : (j + 1) * pair_points] = nt(window, weights)

    for j in range(1, leaves // 2 - 1):
        near_part(j)

    pairs = source.shape[1]
    half = RANK // 2
    wide_target = side_by_side([tgt_ref[...], tgt_ref[...]])
    hits = jnp.where(iota((leaves, 2 * pairs), 0) == wide_target, 1.0, 0.0)
    link_rows = pl_ref[...].reshape(RANK, 2, half, pairs)
    link_rows = jnp.concatenate([link_rows[:, 0], link_rows[:, 1]], axis=2)
    link_high = link_rows.astype(BF16).astype(F32)
    for ref, part in ((pair_high_ref, link_high), (pair_low_ref, link_rows - link_high)):
        for j in range(leaf_blocks):
            hit = hits[j * NODES : (j + 1) * NODES]
            for k in range(half):
                ref[j * LANES : (j + 1) * LANES, k * LANES : (k + 1) * LANES] = jnp.concatenate(
                    [hit * part[a, k : k + 1] for a in range(RANK)], axis=0
                ).astype(BF16)

    pl.when(jnp.logical_not(soon))(exchange)

    for (there, _), copy in zip([sides[1], sides[0], sides[3], sides[2]], side_copies):
        pl.when(there)(copy.wait_recv)

    @pl.when(jnp.logical_not(before))
    def _():
        x_ref[:, 0:halo] = jnp.zeros((vectors, halo), BF16)

    @pl.when(jnp.logical_not(after))
    def _():
        x_ref[:, halo + points :] = jnp.zeros((vectors, halo), BF16)

    @pl.when(jnp.logical_not(below))
    def _():
        below_sums[...] = jnp.zeros(below_sums.shape, F32)

    @pl.when(jnp.logical_not(above))
    def _():
        above_sums[...] = jnp.zeros(above_sums.shape, F32)

    near_part(0)
    near_part(leaves // 2 - 1)

    spot = iota((3 * leaves, pairs), 0)
    reads = jnp.where(spot == src_ref[...], 1.0, 0.0)
    reads = jnp.transpose(reads).astype(BF16)
    found = [nn(reads, part) for part in split(ext_ref[...])]
    rights = [[], []]
    for k in range(half):
        for s in range(2):
            tile = found[s][:, k * LANES : (k + 1) * LANES]
            rights[s].append(jnp.concatenate([tile[:, :vectors], tile[:, vectors:]], axis=0))
    rights = [jnp.concatenate(r, axis=0).astype(BF16) for r in rights]
    for j in range(leaf_blocks):
        block = slice(j * LANES, (j + 1) * LANES)
        added = three(nn, (pair_high_ref[block, :], pair_low_ref[block, :]), rights)
        down = local_down_ref[:, block] + jnp.transpose(added)
        cut = slice(j * width, (j + 1) * width)
        acc_ref[:, cut] = acc_ref[:, cut] + picked_by(nn, split(down), basis_blocks[j])

    for copy in member_copies:
        copy.wait_recv()
    member_sums = members_ref[...]
    own_group[...] = three(nn, (to_group_ref[0:RANK, :], to_group_ref[RANK : 2 * RANK, :]), split(member_sums))

    @pl.when(lon >= 0)
    def _():
        for copy in group_copies:
            copy.start()

    member_across = []
    turned_sums = jnp.transpose(members_ref[...])[:vectors]
    for i in range(len(member_paths)):
        part = split(turned_sums[:, i * per_block : (i + 1) * per_block])
        member_across.append(picked_by(nn, part, member_order))
    member_ups = climb(member_across, members, member_e)
    down_here = None
    for block, pick in zip(descend(member_ups, members, member_e, member_v), own_slots()):
        term = picked_by(nn, split(block), pick)
        down_here = term if down_here is None else down_here + term

    for copy in group_copies:
        copy.wait_recv()
    other_sums = jnp.transpose(groups_ref[...])[:vectors]
    down_here = down_here + three(nn, split(other_sums), (map_ref[0], map_ref[1]))
    down_parts = split(down_here)
    lanes3 = iota((vectors, LANES), 1)
    middle = (lanes3 >= RANK) & (lanes3 < 2 * RANK)
    down3 = jnp.where(middle, down_parts[1].astype(F32), down_parts[0].astype(F32))
    down_ref[...] = down3.astype(BF16)

    for copy in member_copies + group_copies:
        copy.wait_send()
    for (there, _), copy in zip(sides, side_copies):
        pl.when(there)(copy.wait_send)


def last_part(acc_ref, final_ref, down_ref, out_ref, held_ref, sems):
    down3 = down_ref[:, : 3 * RANK]
    points = out_ref.shape[1]
    width = points // 4
    copies = []
    for j in range(4):
        cut = slice(j * width, (j + 1) * width)
        held_ref[:, cut] = acc_ref[:, cut] + nn(down3, final_ref[:, cut])
        copy = pltpu.make_async_copy(held_ref.at[:, cut], out_ref.at[:, cut], sems.at[j])
        copy.start()
        copies.append(copy)
    for copy in copies:
        copy.wait()


def split_lon(n_lon):
    members = 16 if n_lon >= 128 else 1 << n_lon.bit_length() // 2
    return n_lon // members, members


def shards(
    n_lat,
    n_lon,
    ensemble,
    leaf_basis,
    near_blocks,
    local_transfer,
    local_coupling,
    upper_transfer,
    upper_coupling,
    pair_source,
    pair_target,
    pair_coupling,
):
    vectors, points = ensemble.shape
    leaves, leaf_points, window = near_blocks.shape
    halo = window // 2 - leaf_points // 2
    groups, members = split_lon(n_lon)
    pairs = pair_source.shape[2]

    def by_node(matrices):
        nodes = matrices.shape[1]
        return jnp.transpose(matrices[0], (1, 2, 0)).reshape(RANK * RANK, nodes)

    member_blocks = max(1, 2 * members // NODES)
    group_blocks = max(1, 2 * groups // NODES)
    blocks = 2 * leaves // NODES + member_blocks + group_blocks
    upper_nodes = upper_transfer.shape[1]
    operands = (
        ensemble,
        leaf_basis,
        near_blocks,
        by_node(local_transfer),
        by_node(local_coupling),
        by_node(upper_transfer),
        by_node(upper_coupling),
        pair_source[0],
        pair_target[0],
        by_node(pair_coupling[0]),
    )
    scratch = [
        ((vectors, points + 2 * halo), BF16),
        ((RANK, points), BF16),
        (near_blocks.shape, BF16),
        ((RANK * RANK, 2 * leaves), F32),
        ((RANK * RANK, 2 * leaves), F32),
        ((RANK * RANK, upper_nodes), F32),
        ((RANK * RANK, upper_nodes), F32),
        ((1, pairs), jnp.int32),
        ((1, pairs), jnp.int32),
        ((RANK * RANK, pairs), F32),
        ((blocks * LANES, LANES), BF16),
        ((blocks * LANES, LANES), BF16),
        ((blocks * LANES, LANES), BF16),
        ((blocks * LANES, LANES), BF16),
        ((leaves // NODES, LANES, NODES * leaf_points), BF16),
        ((vectors, leaves * RANK), F32),
        ((3 * leaves, RANK * vectors), F32),
        ((members * RANK, LANES), F32),
        ((groups * RANK, LANES), F32),
        ((2 * RANK, members * RANK), BF16),
        ((2, groups * RANK, LANES), BF16),
        ((vectors, leaves * RANK), F32),
        ((leaves * RANK, 2 * pairs * RANK // 2), BF16),
        ((leaves * RANK, 2 * pairs * RANK // 2), BF16),
    ]
    whole = pl.BlockSpec(memory_space=pltpu.VMEM)
    kept = pl.pallas_call(
        functools.partial(kernel, (n_lat, groups, members)),
        out_shape=(
            jax.ShapeDtypeStruct((vectors, points), F32),
            jax.ShapeDtypeStruct((3 * RANK, points), BF16),
            jax.ShapeDtypeStruct((vectors, LANES), BF16),
        ),
        in_specs=[pl.BlockSpec(memory_space=pltpu.HBM)] * len(operands),
        out_specs=(whole, whole, whole),
        scratch_shapes=[pltpu.VMEM(shape, dtype) for shape, dtype in scratch]
        + [
            pltpu.SemaphoreType.DMA((len(operands),)),
            pltpu.SemaphoreType.DMA((members + groups + 2,)),
            pltpu.SemaphoreType.DMA((members - 1,)),
            pltpu.SemaphoreType.DMA((groups - 1,)),
            pltpu.SemaphoreType.DMA((4,)),
        ],
        compiler_params=pltpu.CompilerParams(
            collective_id=0, has_side_effects=True, vmem_limit_bytes=40 * 2**20
        ),
        name="h2_tree",
    )(*[pltpu.with_memory_space_constraint(operand, pltpu.HBM) for operand in operands])
    return pl.pallas_call(
        last_part,
        out_shape=jax.ShapeDtypeStruct((vectors, points), F32),
        in_specs=[whole] * 3,
        out_specs=pl.BlockSpec(memory_space=pltpu.HBM),
        scratch_shapes=[pltpu.VMEM((vectors, points), F32), pltpu.SemaphoreType.DMA((4,))],
        compiler_params=pltpu.CompilerParams(vmem_limit_bytes=8 * 2**20),
        name="h2_last",
    )(*kept)


def solution(mesh):
    return jax.shard_map(
        functools.partial(shards, mesh.shape["lat"], mesh.shape["lon"]),
        mesh=mesh,
        in_specs=(
            P(None, ("lat", "lon")),
            P(None, ("lat", "lon")),
            P(("lat", "lon"), None, None),
            P(("lat", "lon"), None, None, None),
            P(("lat", "lon"), None, None, None),
            P("lat", None, None, None),
            P("lat", None, None, None),
            P("lat", "lon", None),
            P("lat", "lon", None),
            P("lat", "lon", None, None, None),
        ),
        out_specs=P(None, ("lat", "lon")),
        check_vma=False,
    )
```

```python
import functools

import jax
import jax.numpy as jnp
from jax import lax
from jax.experimental import pallas as pl
from jax.experimental.pallas import tpu as pltpu
from jax.sharding import PartitionSpec as P

F32 = jnp.float32
BF16 = jnp.bfloat16
RANK = 16
LANES = 128
NODES = 8
MESH = pl.DeviceIdType.MESH


def iota(shape, axis):
    return lax.broadcasted_iota(jnp.int32, shape, axis)


def one_hot(mask):
    return jnp.where(mask, 1.0, 0.0).astype(BF16)


def nn(a, b):
    return lax.dot_general(a, b, (((1,), (0,)), ((), ())), preferred_element_type=F32)


def nt(a, b):
    return lax.dot_general(a, b, (((1,), (1,)), ((), ())), preferred_element_type=F32)


def split(x):
    high = x.astype(BF16)
    return high, (x - high.astype(F32)).astype(BF16)


def three(dot, a, b):
    rows = a[0].shape[0]
    both = dot(jnp.concatenate(a, axis=0), b[0])
    return both[:rows] + (both[rows:] + dot(a[0], b[1]))


def picked_by(dot, a, b):
    rows = a[0].shape[0]
    both = dot(jnp.concatenate(a, axis=0), b)
    return both[:rows] + both[rows:]


def picks(dot, a, b):
    return dot(a, b[0]) + dot(a, b[1])


def side_by_side(parts):
    return jnp.concatenate(parts, axis=1)


def rows_of(refs, first, count):
    return tuple(ref[pl.ds(first * LANES, count * LANES), :] for ref in refs)


def each(low, high, act):
    def step(index, carry):
        act(index)
        return carry

    lax.fori_loop(low, high, step, 0)


def turn_of(index, count):
    return jnp.where(index <= count // 2, jnp.maximum(2 * index - 1, 0), 2 * (count - index))


def index_at(turn, count):
    return jnp.where(turn % 2 == 1, (turn + 1) // 2, jnp.where(turn == 0, 0, count - turn // 2))


def climb(leaves, count, edge):
    ups = {}
    if count < NODES:
        ups[0] = leaves[0]
        if count >= 4:
            ups[0] = ups[0] + three(nn, split(ups[0]), edge(0, 1))
        return ups
    level = count // NODES
    for i, block in enumerate(leaves):
        ups[level + i] = block
    while level > 1:
        for i in range(level // 2, level):
            pair = side_by_side([ups[2 * i], ups[2 * i + 1]])
            ups[i] = three(nn, split(pair), edge(2 * i, 2))
        level //= 2
    return crown(ups, edge)


def crown(ups, edge):
    ups[0] = three(nn, split(ups[1]), edge(1, 1))
    ups[0] = ups[0] + three(nn, split(ups[0]), edge(0, 1))
    return ups


def descend(ups, count, edge, link, across):
    rows = ups[0].shape[0]
    top = three(across, split(ups[0]), link(0, 1))
    if count >= 4:
        slot = iota((rows, LANES), 1) % NODES
        first = jnp.where((slot == 2) | (slot == 3), top, 0.0)
        top = top + three(nt, split(first), edge(0, 1))
    if count < NODES:
        return [top]
    level = [three(across, split(ups[1]), link(1, 1)) + three(nt, split(top), edge(1, 1))]
    while len(level) < count // NODES:
        width = len(level)
        below = []
        for i, block in enumerate(level):
            node = width + i
            both = three(nt, split(block), edge(2 * node, 2))
            for side in range(2):
                child = 2 * node + side
                own = three(across, split(ups[child]), link(child, 1))
                below.append(own + both[:, side * LANES : (side + 1) * LANES])
        level = below
    return level


def paths(count, edge):
    start = one_hot(iota((RANK, LANES), 1) == iota((RANK, LANES), 0) * NODES + 1)
    step = picks(nt, start, edge(0, 1))
    if count >= 4:
        step = three(nt, split(step), edge(0, 1))
    if count < NODES:
        return [step]
    return longer([three(nt, split(step), edge(1, 1))], count, edge)


def longer(level, count, edge):
    while len(level) < count // NODES:
        below = []
        for i, block in enumerate(level):
            both = three(nt, split(block), edge(2 * (len(level) + i), 2))
            below += [both[:, :LANES], both[:, LANES:]]
        level = below
    return level


def stacked(blocks):
    count = blocks
    members = min(count, NODES)
    offset = count if count < NODES else 0
    row = iota((members * RANK, LANES), 0)
    lane = iota((members * RANK, LANES), 1)
    return one_hot(lane == (row % RANK) * NODES + row // RANK + offset)


def operators(turned, masks, edge_refs, block, spread):
    (high, low), mask = turned, masks
    nodes = high.shape[0]
    for half in range(2):
        cut = slice(half * LANES, (half + 1) * LANES)
        both = jnp.concatenate([high[:, cut], low[:, cut]], axis=0)
        for pair in range(NODES // 2):
            wide = nn(both, spread[pair])
            parts = [
                [
                    jnp.where(mask, wide[k * nodes : (k + 1) * nodes, s * LANES : (s + 1) * LANES], 0.0)
                    for s in range(2)
                ]
                for k in range(2)
            ]
            for k in range(2):
                for j in range(nodes // NODES):
                    rows = slice(j * NODES, (j + 1) * NODES)
                    tile = jnp.concatenate([parts[k][0][rows], parts[k][1][rows]], axis=0)
                    start = (block + j) * LANES + (half * NODES + 2 * pair) * NODES
                    edge_refs[k][start : start + 2 * NODES, :] = tile.astype(BF16)


def kernel(
    sizes,
    ensemble,
    basis,
    near,
    local_edge,
    local_link,
    upper_edge,
    upper_link,
    source,
    target,
    pair_link,
    acc_ref,
    final_ref,
    down_ref,
    x_ref,
    basis_ref,
    near_ref,
    le_ref,
    ll_ref,
    ue_ref,
    ul_ref,
    src_ref,
    tgt_ref,
    pl_ref,
    eh_ref,
    el_ref,
    vh_ref,
    vl_ref,
    basis_blocks,
    ups_ref,
    top_ref,
    ext_ref,
    members_ref,
    groups_ref,
    to_group_ref,
    map_ref,
    local_down_ref,
    pair_high_ref,
    pair_low_ref,
    here_ref,
    load_sem,
    member_send,
    group_send,
    stand_in_send,
    side_send,
    member_sem,
    group_sem,
    side_sem,
    member_in,
    group_in,
    side_in,
):
    n_lat, groups, members = sizes
    n_lon = groups * members
    vectors, points = ensemble.shape
    leaves = near.shape[0]
    leaf_points = near.shape[1]
    halo = near.shape[2] // 2 - leaf_points // 2
    lat, lon = lax.axis_index("lat"), lax.axis_index("lon")
    group, member = lon // members, lax.rem(lon, members)
    flat = lat * n_lon + lon
    total = n_lat * n_lon

    member_shift = jnp.where((lat == 0) & (group == 0), 1, 0)
    group_shift = jnp.where((lat == 0) & (member == 0), 1, 0)
    cores = min(members, 2)
    lines = members // cores
    member_turn = turn_of(member // cores, lines) * cores + lax.rem(member, cores)
    member_turn = lax.rem(member_turn + members - member_shift, members)
    group_turn = lax.rem(turn_of(group, groups) + groups - group_shift, groups)

    def member_by(turn):
        turn = lax.rem(turn + member_shift, members)
        return index_at(turn // cores, lines) * cores + lax.rem(turn, cores)

    def group_by(turn):
        return index_at(lax.rem(turn + group_shift, groups), groups)

    def member_at(j):
        return (lat, group * members + j)

    def group_at(j):
        return (lat, j * members + member)

    after, before = flat < total - 1, flat > 0
    above, below = lat < n_lat - 1, lat > 0
    after_at = ((flat + 1) // n_lon, lax.rem(flat + 1, n_lon))
    before_at = ((flat - 1) // n_lon, lax.rem(flat + total - 1, n_lon))
    above_at, below_at = (lat + 1, lon), (lat - 1, lon)
    earlier = [after & (flat == 0), before & (flat != 1), above & (flat == 0), below & (flat != n_lon)]
    later = [after & (flat != 0), before & (flat == 1), above & (flat != 0), below & (flat == n_lon)]
    beside_at = [after_at, before_at, above_at, below_at]
    mirror = [1, 0, 3, 2]

    own_points = x_ref.at[:, halo : halo + points]
    loads = [
        pltpu.make_async_copy(src, dst, load_sem.at[i])
        for i, (src, dst) in enumerate(
            [
                (local_edge, le_ref),
                (basis, basis_ref),
                (ensemble, own_points),
                (local_link, ll_ref),
                (upper_edge, ue_ref),
                (upper_link, ul_ref),
                (source, src_ref),
                (target, tgt_ref),
                (pair_link, pl_ref),
                (near, near_ref),
            ]
        )
    ]
    for load in loads:
        load.start()

    barrier = pltpu.get_barrier_semaphore()

    def signal(semaphore, peer):
        pl.semaphore_signal(semaphore, inc=1, device_id=peer, device_id_type=MESH)

    each(member_turn + 1, members, lambda t: signal(barrier, member_at(member_by(t))))
    each(group_turn + 1, groups, lambda t: signal(barrier, group_at(group_by(t))))
    for there, peer in zip(later, beside_at):
        pl.when(there)(functools.partial(signal, barrier, peer))
    stand_in = flat == 1
    stood_for = (lat == 0) & (member == 0) & (group > 0)
    pl.when(stood_for)(lambda: signal(barrier, (lat, 1)))

    heard = member_turn + group_turn + jnp.where(stand_in, groups - 1, 0)
    for there in earlier:
        heard = heard + jnp.where(there, 1, 0)
    pl.semaphore_wait(barrier, heard)
    each(0, member_turn, lambda t: signal(member_in.at[member], member_at(member_by(t))))
    each(0, group_turn, lambda t: signal(group_in.at[group], group_at(group_by(t))))
    for k in range(4):
        pl.when(earlier[k])(functools.partial(signal, side_in.at[mirror[k]], beside_at[k]))

    row, lane = iota((LANES, LANES), 0), iota((LANES, LANES), 1)
    offset = row - lane // NODES
    spread = []
    for pair in range(NODES // 2):
        spread.append(
            side_by_side([one_hot(offset == (2 * pair + s) * RANK) for s in range(2)])
        )

    def masks(count, slots):
        node_slot = slots(iota((count, LANES), 0))
        column = iota((count, LANES), 1) % NODES
        inner = node_slot >= 2
        edge = inner & (column == (node_slot // 2) % NODES)
        link = inner & (column == (node_slot + 1 - 2 * (node_slot % 2)) % NODES)
        return edge, link

    eye = one_hot(iota((2 * leaves, 2 * leaves), 0) == iota((2 * leaves, 2 * leaves), 1))
    local_masks = masks(2 * leaves, lambda r: r)

    def turned(ref, chosen):
        parts = split(ref[...])
        return tuple(nt(chosen, part).astype(BF16) for part in parts)

    edges, links = (eh_ref, el_ref), (vh_ref, vl_ref)
    local_blocks = 2 * leaves // NODES
    member_blocks = max(1, 2 * members // NODES)
    group_blocks = max(1, 2 * groups // NODES)

    def reader(refs, base):
        return lambda first, count: rows_of(refs, base + first, count)

    local_e, local_v = reader(edges, 0), reader(links, 0)
    member_e, member_v = reader(edges, local_blocks), reader(links, local_blocks)
    group_base = local_blocks + member_blocks
    group_e, group_v = reader(edges, group_base), reader(links, group_base)

    for load in loads[:3]:
        load.wait()
    operators(turned(le_ref, eye), local_masks[0], edges, 0, spread)
    width = NODES * leaf_points
    leaf_blocks = leaves // NODES
    keep = iota((NODES, width), 0) == iota((NODES, width), 1) // leaf_points
    for j in range(leaf_blocks):
        part = basis_ref[:, j * width : (j + 1) * width].astype(F32)
        for k in range(0, RANK, 2):
            tiles = [
                jnp.where(keep, jnp.broadcast_to(part[k + s : k + s + 1], (NODES, width)), 0.0)
                for s in range(2)
            ]
            basis_blocks[j, k * NODES : (k + 2) * NODES, :] = jnp.concatenate(tiles, axis=0).astype(BF16)
    across = []
    for j in range(leaf_blocks):
        x_part = x_ref[:, halo + j * width : halo + (j + 1) * width]
        across.append(nt(x_part, basis_blocks[j]))
    top = paths(NODES, local_e)[0]
    halves = [
        three(nn, split(side_by_side([across[2 * i], across[2 * i + 1]])), local_e(leaf_blocks + 2 * i, 2))
        for i in range(leaf_blocks // 2)
    ]
    eighth = three(nn, split(side_by_side(halves)), local_e(2, 2))
    device_sum = three(nt, split(top), split(eighth))
    top_ref[...] = top
    for i, block in enumerate([eighth] + halves + across):
        ups_ref[:, i * LANES : (i + 1) * LANES] = block
    empty = jnp.zeros((RANK, LANES - vectors), F32)
    own_member = members_ref.at[pl.ds(member * RANK, RANK)]
    own_member[...] = side_by_side([device_sum, empty])

    def copy_to(src, dst, sent, arrived, peer):
        return pltpu.make_async_remote_copy(
            src_ref=src,
            dst_ref=dst,
            send_sem=sent,
            recv_sem=arrived,
            device_id=peer,
            device_id_type=MESH,
        )

    def member_copy(j):
        return copy_to(own_member, own_member, member_send.at[j], member_sem.at[member], member_at(j))

    def member_arrival(j):
        there = members_ref.at[pl.ds(j * RANK, RANK)]
        return copy_to(there, there, member_send.at[j], member_sem.at[j], member_at(j))

    own_group = groups_ref.at[pl.ds(group * RANK, RANK)]

    def group_copy(j):
        return copy_to(own_group, own_group, group_send.at[j], group_sem.at[group], group_at(j))

    def stand_in_copy(j):
        return copy_to(own_group, own_group, stand_in_send.at[j], group_sem.at[0], (lat, j * members))

    def group_arrival(j):
        there = groups_ref.at[pl.ds(j * RANK, RANK)]
        return copy_to(there, there, group_send.at[j], group_sem.at[j], group_at(j))

    own_sums = ext_ref.at[leaves : 2 * leaves]
    first_halo, last_halo = x_ref.at[:, halo : 2 * halo], x_ref.at[:, points : points + halo]
    left_halo, right_halo = x_ref.at[:, 0:halo], x_ref.at[:, halo + points : points + 2 * halo]
    below_sums, above_sums = ext_ref.at[0:leaves], ext_ref.at[2 * leaves : 3 * leaves]
    to_after = copy_to(last_halo, left_halo, side_send.at[0], side_sem.at[0], after_at)
    to_before = copy_to(first_halo, right_halo, side_send.at[1], side_sem.at[1], before_at)
    to_above = copy_to(own_sums, below_sums, side_send.at[2], side_sem.at[2], above_at)
    to_below = copy_to(own_sums, above_sums, side_send.at[3], side_sem.at[3], below_at)
    from_before, from_after, from_below, from_above = to_after, to_before, to_above, to_below
    side_copies = [to_after, to_before, to_above, to_below]

    def to_member(j):
        pl.semaphore_wait(member_in.at[j], 1)
        member_copy(j).start()

    def to_group(j):
        pl.semaphore_wait(group_in.at[j], 1)
        group_copy(j).start()

    def to_side(k):
        pl.semaphore_wait(side_in.at[k], 1)
        side_copies[k].start()

    each(0, member_turn, lambda t: member_copy(member_by(member_turn - 1 - t)).start())
    for k in range(2):
        pl.when(earlier[k])(side_copies[k].start)

    for j in range(leaf_blocks):
        x_part = x_ref[:, halo + j * width : halo + (j + 1) * width]
        by_rank = nt(basis_blocks[j], x_part)
        for k in range(RANK // 2):
            ext_ref[leaves + j * NODES : leaves + (j + 1) * NODES, k * LANES : (k + 1) * LANES] = side_by_side(
                [
                    by_rank[k * NODES : (k + 1) * NODES],
                    by_rank[(k + RANK // 2) * NODES : (k + RANK // 2 + 1) * NODES],
                ]
            )

    for k in range(2, 4):
        pl.when(earlier[k])(side_copies[k].start)

    member_slots, group_slots = member_blocks * NODES, group_blocks * NODES
    upper_rows = member_slots + group_slots
    upper_nodes = upper_edge.shape[1]
    slot = iota((upper_rows, upper_nodes), 0)
    scale = jnp.where(slot >= 2, 2, 1)
    for power in range(2, members.bit_length()):
        scale = jnp.where(slot >= 2**power, 2**power, scale)
    wanted = jnp.where(slot < member_slots, slot + (groups + group - 1) * scale, slot - member_slots)
    chosen = one_hot(wanted == iota((upper_rows, upper_nodes), 1))
    upper_masks = masks(upper_rows, lambda r: jnp.where(r < member_slots, r, r - member_slots))
    loads[4].wait()
    operators(turned(ue_ref, chosen), upper_masks[0], edges, local_blocks, spread)

    per_block = min(members, NODES) * RANK
    member_order = stacked(members)
    member_paths = paths(members, member_e)
    for i, block in enumerate(member_paths):
        cut = slice(i * per_block, (i + 1) * per_block)
        high, low = split(picked_by(nt, split(block), member_order))
        to_group_ref[0:RANK, cut] = high
        to_group_ref[RANK : 2 * RANK, cut] = low

    blank = jnp.zeros((leaf_points, leaf_points), BF16)
    pair_points = 2 * leaf_points
    span = near.shape[2] + leaf_points
    pairs = source.shape[1]
    half = RANK // 2

    def near_part(j, low, high, add):
        first = side_by_side([near_ref[2 * j], blank])
        second = side_by_side([blank, near_ref[2 * j + 1]])
        weights = jnp.concatenate([first, second], axis=0)[:, low:high]
        window = x_ref[:, j * pair_points + low : j * pair_points + high]
        cut = slice(j * pair_points, (j + 1) * pair_points)
        part = nt(window, weights)
        acc_ref[:, cut] = acc_ref[:, cut] + part if add else part

    def local_work():
        for load in loads[3:4] + loads[5:]:
            load.wait()
        operators(turned(ul_ref, chosen), upper_masks[1], links, local_blocks, spread)
        operators(turned(ll_ref, eye), local_masks[1], links, 0, spread)

        own_rows, own_lanes = iota((RANK, LANES), 0), iota((RANK, LANES), 1)
        starts = []
        for i in range(len(member_paths)):
            mine = member - i * NODES if members >= NODES else member + members
            inside = (mine >= 0) & (mine < NODES)
            starts.append(jnp.where((own_lanes == own_rows * NODES + mine) & inside, 1.0, 0.0))
        member_ups = climb(starts, members, member_e)
        group_slot = group if groups >= NODES else group + groups
        place = one_hot((row // NODES == lane // NODES) & (row % NODES == 1) & (lane % NODES == group_slot))
        placed = picked_by(nn, split(three(nn, split(member_ups[0]), member_e(0, 1))), place)
        group_ups = climb([placed], groups, group_e)
        maps = [
            picked_by(nt, split(block), member_order)
            for block in descend(member_ups, members, member_e, member_v, nn)
        ]
        maps.append(picked_by(nt, split(descend(group_ups, groups, group_e, group_v, nn)[0]), stacked(groups)))
        for i, part in enumerate(split(side_by_side(maps))):
            map_ref[i] = jnp.concatenate([part] * 3, axis=0)

        local_ups = {i + 1: ups_ref[:, i * LANES : (i + 1) * LANES] for i in range(2 * leaf_blocks - 1)}
        for j, block in enumerate(descend(crown(local_ups, local_e), leaves, local_e, local_v, nt)):
            local_down_ref[:, j * LANES : (j + 1) * LANES] = block
        for j, block in enumerate(longer([top_ref[...]], leaves, local_e)):
            folded = split(picked_by(nn, split(block), basis_blocks[j]))
            cut = slice(j * width, (j + 1) * width)
            final_ref[0:RANK, cut] = folded[0]
            final_ref[RANK : 2 * RANK, cut] = folded[0]
            final_ref[2 * RANK : 3 * RANK, cut] = folded[1]

        for j in range(leaves // 2):
            low, high = (halo if j == 0 else 0), (span - halo if j == leaves // 2 - 1 else span)
            near_part(j, low, high, False)

        wide_target = side_by_side([tgt_ref[...], tgt_ref[...]])
        hits = jnp.where(iota((leaves, 2 * pairs), 0) == wide_target, 1.0, 0.0)
        link_rows = pl_ref[...].reshape(RANK, 2, half, pairs)
        link_rows = jnp.concatenate([link_rows[:, 0], link_rows[:, 1]], axis=2)
        link_high = link_rows.astype(BF16).astype(F32)
        for ref, part in ((pair_high_ref, link_high), (pair_low_ref, link_rows - link_high)):
            for j in range(leaf_blocks):
                hit = hits[j * NODES : (j + 1) * NODES]
                for k in range(half):
                    ref[j * LANES : (j + 1) * LANES, k * LANES : (k + 1) * LANES] = jnp.concatenate(
                        [hit * part[a, k : k + 1] for a in range(RANK)], axis=0
                    ).astype(BF16)

    for k in (0, 2):
        pl.when(later[k])(functools.partial(to_side, k))

    def late_sends():
        each(member_turn + 1, members - member_shift, lambda t: to_member(member_by(t)))

    def beside():
        for k in (1, 3):
            pl.when(later[k])(functools.partial(to_side, k))

        pl.when(below)(from_below.wait_recv)
        pl.when(above)(from_above.wait_recv)

        @pl.when(jnp.logical_not(below))
        def _():
            below_sums[...] = jnp.zeros(below_sums.shape, F32)

        @pl.when(jnp.logical_not(above))
        def _():
            above_sums[...] = jnp.zeros(above_sums.shape, F32)

        spot = iota((3 * leaves, pairs), 0)
        reads = jnp.where(spot == src_ref[...], 1.0, 0.0)
        reads = jnp.transpose(reads).astype(BF16)
        found = [nn(reads, part) for part in split(ext_ref[...])]
        left_side = iota((pairs, LANES), 1) < vectors
        rights = []
        for k in range(half):
            high, low = (part[:, k * LANES : (k + 1) * LANES] for part in found)
            rights.append(jnp.where(left_side, high, pltpu.roll(low, vectors, 1)))
            rights.append(jnp.where(left_side, pltpu.roll(high, vectors, 1), low))
        rights = jnp.concatenate(rights, axis=0).astype(BF16)
        for j in range(leaf_blocks):
            block = slice(j * LANES, (j + 1) * LANES)
            high_both = nn(pair_high_ref[block, :], rights)
            added = high_both[:, :vectors] + (high_both[:, vectors:] + nn(pair_low_ref[block, :], rights[:, :vectors]))
            down = local_down_ref[:, block] + jnp.transpose(added)
            cut = slice(j * width, (j + 1) * width)
            acc_ref[:, cut] = acc_ref[:, cut] + picked_by(nn, split(down), basis_blocks[j])

        pl.when(before)(from_before.wait_recv)
        pl.when(after)(from_after.wait_recv)

        @pl.when(jnp.logical_not(before))
        def _():
            left_halo[...] = jnp.zeros((vectors, halo), BF16)

        @pl.when(jnp.logical_not(after))
        def _():
            right_halo[...] = jnp.zeros((vectors, halo), BF16)

        near_part(0, 0, halo, True)
        near_part(leaves // 2 - 1, span - halo, span, True)

    def relay():
        @pl.when((member_shift == 1) & (member_turn < members - 1))
        def _():
            to_member(0)

        each(0, member, lambda j: member_arrival(j).wait_recv())
        each(member + 1, members, lambda j: member_arrival(j).wait_recv())
        own_group[...] = three(
            nn, (to_group_ref[0:RANK, :], to_group_ref[RANK : 2 * RANK, :]), split(members_ref[...])
        )
        @pl.when(flat > 0)
        def _():
            each(0, group_turn, lambda t: group_copy(group_by(group_turn - 1 - t)).start())

        @pl.when(stand_in)
        def _():
            each(1, groups, lambda j: stand_in_copy(j).start())

        each(group_turn + 1, groups, lambda t: to_group(group_by(t)))

    def stage(step, carry):
        turn = jnp.where((lat == 0) | (step == 0), step, 3 - step)
        pl.when(turn == 0)(local_work)
        pl.when(step == 0)(late_sends)
        pl.when(turn == 1)(beside)
        pl.when(turn == 2)(relay)
        return carry

    lax.fori_loop(0, 3, stage, 0)

    def mapped(ref, first, count):
        cut = slice(first * RANK, (first + count) * RANK)
        turned_sums = jnp.transpose(ref[...])[:vectors]
        return three(nt, split(turned_sums), (map_ref[0][:, cut], map_ref[1][:, cut]))

    here_ref[...] = mapped(members_ref, 0, members)
    each(0, group, lambda j: group_arrival(j).wait_recv())
    each(group + 1, groups, lambda j: group_arrival(j).wait_recv())
    down_here = here_ref[...] + mapped(groups_ref, members, groups)
    down_parts = split(down_here)
    lanes3 = iota(down_here.shape, 1)
    middle = (lanes3 >= RANK) & (lanes3 < 2 * RANK)
    down3 = jnp.where(middle, down_parts[1].astype(F32), down_parts[0].astype(F32))
    down_ref[...] = down3.astype(BF16)

    each(0, member, lambda j: member_copy(j).wait_send())
    each(member + 1, members, lambda j: member_copy(j).wait_send())

    @pl.when(flat > 0)
    def _():
        each(0, group, lambda j: group_copy(j).wait_send())
        each(group + 1, groups, lambda j: group_copy(j).wait_send())

    @pl.when(stand_in)
    def _():
        each(1, groups, lambda j: stand_in_copy(j).wait_send())

    pl.when(after)(to_after.wait_send)
    pl.when(before)(to_before.wait_send)
    pl.when(above)(to_above.wait_send)
    pl.when(below)(to_below.wait_send)


def last_part(acc_ref, final_ref, down_ref, out_ref, held_ref, sems):
    down3 = down_ref[...]
    points = out_ref.shape[1]
    width = points // 4
    copies = []
    for j in range(4):
        cut = slice(j * width, (j + 1) * width)
        held_ref[:, cut] = acc_ref[:, cut] + nn(down3, final_ref[:, cut])
        copy = pltpu.make_async_copy(held_ref.at[:, cut], out_ref.at[:, cut], sems.at[j])
        copy.start()
        copies.append(copy)
    for copy in copies:
        copy.wait()


def split_lon(n_lon):
    members = 16 if n_lon >= 128 else 1 << n_lon.bit_length() // 2
    return n_lon // members, members


def shards(
    n_lat,
    n_lon,
    ensemble,
    leaf_basis,
    near_blocks,
    local_transfer,
    local_coupling,
    upper_transfer,
    upper_coupling,
    pair_source,
    pair_target,
    pair_coupling,
):
    vectors, points = ensemble.shape
    leaves, leaf_points, window = near_blocks.shape
    halo = window // 2 - leaf_points // 2
    groups, members = split_lon(n_lon)
    pairs = pair_source.shape[2]

    def by_node(matrices):
        nodes = matrices.shape[1]
        return jnp.transpose(matrices[0], (1, 2, 0)).reshape(RANK * RANK, nodes)

    member_blocks = max(1, 2 * members // NODES)
    group_blocks = max(1, 2 * groups // NODES)
    blocks = 2 * leaves // NODES + member_blocks + group_blocks
    upper_nodes = upper_transfer.shape[1]
    operands = (
        ensemble,
        leaf_basis,
        near_blocks,
        by_node(local_transfer),
        by_node(local_coupling),
        by_node(upper_transfer),
        by_node(upper_coupling),
        pair_source[0],
        pair_target[0],
        by_node(pair_coupling[0]),
    )
    scratch = [
        ((vectors, points + 2 * halo), BF16),
        ((RANK, points), BF16),
        (near_blocks.shape, BF16),
        ((RANK * RANK, 2 * leaves), F32),
        ((RANK * RANK, 2 * leaves), F32),
        ((RANK * RANK, upper_nodes), F32),
        ((RANK * RANK, upper_nodes), F32),
        ((1, pairs), jnp.int32),
        ((1, pairs), jnp.int32),
        ((RANK * RANK, pairs), F32),
        ((blocks * LANES, LANES), BF16),
        ((blocks * LANES, LANES), BF16),
        ((blocks * LANES, LANES), BF16),
        ((blocks * LANES, LANES), BF16),
        ((leaves // NODES, LANES, NODES * leaf_points), BF16),
        ((vectors, (2 * leaves // NODES - 1) * LANES), F32),
        ((RANK, LANES), F32),
        ((3 * leaves, RANK * vectors), F32),
        ((members * RANK, LANES), F32),
        ((groups * RANK, LANES), F32),
        ((2 * RANK, members * RANK), BF16),
        ((2, 3 * RANK, (members + groups) * RANK), BF16),
        ((vectors, leaves * RANK), F32),
        ((leaves * RANK, 2 * pairs * RANK // 2), BF16),
        ((leaves * RANK, 2 * pairs * RANK // 2), BF16),
        ((vectors, 3 * RANK), F32),
    ]
    whole = pl.BlockSpec(memory_space=pltpu.VMEM)
    kept = pl.pallas_call(
        functools.partial(kernel, (n_lat, groups, members)),
        out_shape=(
            jax.ShapeDtypeStruct((vectors, points), F32),
            jax.ShapeDtypeStruct((3 * RANK, points), BF16),
            jax.ShapeDtypeStruct((vectors, 3 * RANK), BF16),
        ),
        in_specs=[pl.BlockSpec(memory_space=pltpu.HBM)] * len(operands),
        out_specs=(whole, whole, whole),
        scratch_shapes=[pltpu.VMEM(shape, dtype) for shape, dtype in scratch]
        + [
            pltpu.SemaphoreType.DMA((len(operands),)),
            pltpu.SemaphoreType.DMA((members,)),
            pltpu.SemaphoreType.DMA((groups,)),
            pltpu.SemaphoreType.DMA((groups,)),
            pltpu.SemaphoreType.DMA((4,)),
            pltpu.SemaphoreType.DMA((members,)),
            pltpu.SemaphoreType.DMA((groups,)),
            pltpu.SemaphoreType.DMA((4,)),
            pltpu.SemaphoreType.REGULAR((members,)),
            pltpu.SemaphoreType.REGULAR((groups,)),
            pltpu.SemaphoreType.REGULAR((4,)),
        ],
        compiler_params=pltpu.CompilerParams(
            collective_id=0, has_side_effects=True, vmem_limit_bytes=40 * 2**20
        ),
        name="h2_tree",
    )(*[pltpu.with_memory_space_constraint(operand, pltpu.HBM) for operand in operands])
    return pl.pallas_call(
        last_part,
        out_shape=jax.ShapeDtypeStruct((vectors, points), F32),
        in_specs=[whole] * 3,
        out_specs=pl.BlockSpec(memory_space=pltpu.HBM),
        scratch_shapes=[pltpu.VMEM((vectors, points), F32), pltpu.SemaphoreType.DMA((4,))],
        compiler_params=pltpu.CompilerParams(vmem_limit_bytes=8 * 2**20),
        name="h2_last",
    )(*kept)


def solution(mesh):
    return jax.shard_map(
        functools.partial(shards, mesh.shape["lat"], mesh.shape["lon"]),
        mesh=mesh,
        in_specs=(
            P(None, ("lat", "lon")),
            P(None, ("lat", "lon")),
            P(("lat", "lon"), None, None),
            P(("lat", "lon"), None, None, None),
            P(("lat", "lon"), None, None, None),
            P("lat", None, None, None),
            P("lat", None, None, None),
            P("lat", "lon", None),
            P("lat", "lon", None),
            P("lat", "lon", None, None, None),
        ),
        out_specs=P(None, ("lat", "lon")),
        check_vma=False,
    )
```

```python
import functools

import jax
import jax.numpy as jnp
from jax import lax
from jax.experimental import pallas as pl
from jax.experimental.pallas import tpu as pltpu
from jax.sharding import PartitionSpec as P

F32 = jnp.float32
BF16 = jnp.bfloat16
RANK = 16
LANES = 128
HALF = RANK // 2
NODES = 8
MESH = pl.DeviceIdType.MESH


def iota(shape, axis):
    return lax.broadcasted_iota(jnp.int32, shape, axis)


def one_hot(mask):
    return jnp.where(mask, 1.0, 0.0).astype(BF16)


def nn(a, b):
    return lax.dot_general(a, b, (((1,), (0,)), ((), ())), preferred_element_type=F32)


def nt(a, b):
    return lax.dot_general(a, b, (((1,), (1,)), ((), ())), preferred_element_type=F32)


def split(x):
    high = x.astype(BF16)
    return high, (x - high.astype(F32)).astype(BF16)


def three(dot, a, b):
    rows = a[0].shape[0]
    both = dot(jnp.concatenate(a, axis=0), b[0])
    return both[:rows] + (both[rows:] + dot(a[0], b[1]))


def picked_by(dot, a, b):
    rows = a[0].shape[0]
    both = dot(jnp.concatenate(a, axis=0), b)
    return both[:rows] + both[rows:]


def picks(dot, a, b):
    return dot(a, b[0]) + dot(a, b[1])


def side_by_side(parts):
    return jnp.concatenate(parts, axis=1)


def rows_of(refs, first, count):
    return tuple(ref[pl.ds(first * LANES, count * LANES), :] for ref in refs)


def each(count, wanted, act):
    for turn in range(count):
        pl.when(wanted(turn))(functools.partial(act, turn))


def wait(semaphore, count):
    pl.when(count > 0)(lambda: pl.semaphore_wait(semaphore, count))


def turn_of(index, count):
    return jnp.where(index <= count // 2, jnp.maximum(2 * index - 1, 0), 2 * (count - index))


def index_at(turn, count):
    return jnp.where(turn % 2 == 1, (turn + 1) // 2, jnp.where(turn == 0, 0, count - turn // 2))


def climb(leaves, count, edge):
    ups = {}
    if count < NODES:
        ups[0] = leaves[0]
        if count >= 4:
            ups[0] = ups[0] + three(nn, split(ups[0]), edge(0, 1))
        return ups
    level = count // NODES
    for i, block in enumerate(leaves):
        ups[level + i] = block
    while level > 1:
        for i in range(level // 2, level):
            pair = side_by_side([ups[2 * i], ups[2 * i + 1]])
            ups[i] = three(nn, split(pair), edge(2 * i, 2))
        level //= 2
    return crown(ups, edge)


def crown(ups, edge):
    ups[0] = three(nn, split(ups[1]), edge(1, 1))
    ups[0] = ups[0] + three(nn, split(ups[0]), edge(0, 1))
    return ups


def descend(ups, count, edge, link, across):
    rows = ups[0].shape[0]
    top = three(across, split(ups[0]), link(0, 1))
    if count >= 4:
        slot = iota((rows, LANES), 1) % NODES
        first = jnp.where((slot == 2) | (slot == 3), top, 0.0)
        top = top + three(nt, split(first), edge(0, 1))
    if count < NODES:
        return [top]
    level = [three(across, split(ups[1]), link(1, 1)) + three(nt, split(top), edge(1, 1))]
    while len(level) < count // NODES:
        width = len(level)
        below = []
        for i, block in enumerate(level):
            node = width + i
            both = three(nt, split(block), edge(2 * node, 2))
            for side in range(2):
                child = 2 * node + side
                own = three(across, split(ups[child]), link(child, 1))
                below.append(own + both[:, side * LANES : (side + 1) * LANES])
        level = below
    return level


def paths(count, edge):
    start = one_hot(iota((RANK, LANES), 1) == iota((RANK, LANES), 0) * NODES + 1)
    step = picks(nt, start, edge(0, 1))
    if count >= 4:
        step = three(nt, split(step), edge(0, 1))
    if count < NODES:
        return [step]
    return longer([three(nt, split(step), edge(1, 1))], count, edge)


def longer(level, count, edge):
    while len(level) < count // NODES:
        below = []
        for i, block in enumerate(level):
            both = three(nt, split(block), edge(2 * (len(level) + i), 2))
            below += [both[:, :LANES], both[:, LANES:]]
        level = below
    return level


def stacked(count, half):
    members = min(count, NODES)
    offset = count if count < NODES else 0
    row = iota((members * HALF, LANES), 0)
    lane = iota((members * HALF, LANES), 1)
    return one_hot(lane == (half * HALF + row % HALF) * NODES + row // HALF + offset)


def operators(turned, masks, edge_refs, block, spread):
    (high, low), mask = turned, masks
    nodes = high.shape[0]
    for half in range(2):
        cut = slice(half * LANES, (half + 1) * LANES)
        both = jnp.concatenate([high[:, cut], low[:, cut]], axis=0)
        for pair in range(NODES // 2):
            wide = nn(both, spread[pair])
            parts = [
                [
                    jnp.where(mask, wide[k * nodes : (k + 1) * nodes, s * LANES : (s + 1) * LANES], 0.0)
                    for s in range(2)
                ]
                for k in range(2)
            ]
            for k in range(2):
                for j in range(nodes // NODES):
                    rows = slice(j * NODES, (j + 1) * NODES)
                    tile = jnp.concatenate([parts[k][0][rows], parts[k][1][rows]], axis=0)
                    start = (block + j) * LANES + (half * NODES + 2 * pair) * NODES
                    edge_refs[k][start : start + 2 * NODES, :] = tile.astype(BF16)


def kernel(
    sizes,
    ensemble,
    basis,
    near,
    local_edge,
    local_link,
    upper_edge,
    upper_link,
    source,
    target,
    pair_link,
    acc_ref,
    final_ref,
    down_ref,
    x_ref,
    basis_ref,
    near_ref,
    le_ref,
    linked_ref,
    upper_ref,
    pairs_ref,
    eh_ref,
    el_ref,
    vh_ref,
    vl_ref,
    basis_blocks,
    ups_ref,
    top_ref,
    ext_ref,
    members_ref,
    groups_ref,
    to_group_ref,
    map_ref,
    local_down_ref,
    pair_high_ref,
    pair_low_ref,
    here_ref,
    load_sem,
    member_send,
    group_send,
    stand_in_send,
    side_send,
    member_sem,
    group_sem,
    side_sem,
    member_in,
    group_in,
    side_in,
    last_in,
):
    n_lat, groups, members = sizes
    n_lon = groups * members
    vectors, points = ensemble.shape
    leaves = near.shape[0]
    leaf_points = near.shape[1]
    halo = near.shape[2] // 2 - leaf_points // 2
    lat, lon = lax.axis_index("lat"), lax.axis_index("lon")
    group, member = lon // members, lax.rem(lon, members)
    flat = lat * n_lon + lon
    total = n_lat * n_lon

    member_shift = jnp.where((lat == 0) & (group == 0), 1, 0)
    group_shift = jnp.where((lat == 0) & (member == 0), 1, 0)
    cores = min(members, 2)
    lines = members // cores
    member_turn = turn_of(member // cores, lines) * cores + lax.rem(member, cores)
    member_turn = lax.rem(member_turn + members - member_shift, members)
    group_turn = lax.rem(turn_of(group, groups) + groups - group_shift, groups)

    def member_by(turn):
        turn = lax.rem(turn + member_shift, members)
        return index_at(turn // cores, lines) * cores + lax.rem(turn, cores)

    def group_by(turn):
        return index_at(lax.rem(turn + group_shift, groups), groups)

    def member_at(j):
        return (lat, group * members + j)

    def group_at(j):
        return (lat, j * members + member)

    after, before = flat < total - 1, flat > 0
    above, below = lat < n_lat - 1, lat > 0
    after_at = ((flat + 1) // n_lon, lax.rem(flat + 1, n_lon))
    before_at = ((flat - 1) // n_lon, lax.rem(flat + total - 1, n_lon))
    above_at, below_at = (lat + 1, lon), (lat - 1, lon)
    earlier = [after & (flat == 0), before & (flat != 1), above & (flat == 0), below & (flat != n_lon)]
    later = [after & (flat != 0), before & (flat == 1), above & (flat != 0), below & (flat == n_lon)]
    beside_at = [after_at, before_at, above_at, below_at]
    mirror = [1, 0, 3, 2]

    own_points = x_ref.at[:, halo : halo + points]
    sources = [
        (0, local_edge, le_ref),
        (1, basis, basis_ref),
        (2, ensemble, own_points),
        (3, upper_edge, upper_ref.at[0]),
        (3, upper_link, upper_ref.at[1]),
        (4, local_link, linked_ref.at[0]),
        (4, pair_link, linked_ref.at[1]),
        (5, source, pairs_ref.at[0]),
        (5, target, pairs_ref.at[1]),
        (6, near, near_ref),
    ]
    for i, src, dst in sources:
        pltpu.make_async_copy(src, dst, load_sem.at[i]).start()

    def loaded(i, ref):
        pltpu.make_async_copy(ref, ref, load_sem.at[i]).wait()

    barrier = pltpu.get_barrier_semaphore()

    def signal(semaphore, peer):
        pl.semaphore_signal(semaphore, inc=1, device_id=peer, device_id_type=MESH)

    each(members, lambda t: t > member_turn, lambda t: signal(barrier, member_at(member_by(t))))
    each(groups, lambda t: t > group_turn, lambda t: signal(barrier, group_at(group_by(t))))
    for there, peer in zip(later, beside_at):
        pl.when(there)(functools.partial(signal, barrier, peer))
    stand_in = flat == 1
    stood_for = (lat == 0) & (member == 0) & (group > 0)
    pl.when(stood_for)(lambda: signal(barrier, (lat, 1)))

    heard = member_turn + group_turn + jnp.where(stand_in, groups - 1, 0)
    for there in earlier:
        heard = heard + jnp.where(there, 1, 0)
    wait(barrier, heard)
    is_last = flat == 0

    @pl.when(is_last)
    def _():
        for j in range(1, members):
            signal(last_in, member_at(j))
        pl.when(above)(lambda: signal(last_in, above_at))

    @pl.when(flat > 0)
    def _():
        each(members, lambda t: t < member_turn, lambda t: signal(member_in, member_at(member_by(t))))
        for k in range(4):
            pl.when(earlier[k])(functools.partial(signal, side_in, beside_at[k]))

    each(groups, lambda t: t < group_turn, lambda t: signal(group_in, group_at(group_by(t))))

    row, lane = iota((LANES, LANES), 0), iota((LANES, LANES), 1)
    offset = row - lane // NODES
    spread = []
    for pair in range(NODES // 2):
        spread.append(
            side_by_side([one_hot(offset == (2 * pair + s) * RANK) for s in range(2)])
        )

    def masks(count, slots):
        node_slot = slots(iota((count, LANES), 0))
        column = iota((count, LANES), 1) % NODES
        inner = node_slot >= 2
        edge = inner & (column == (node_slot // 2) % NODES)
        link = inner & (column == (node_slot + 1 - 2 * (node_slot % 2)) % NODES)
        return edge, link

    eye = one_hot(iota((2 * leaves, 2 * leaves), 0) == iota((2 * leaves, 2 * leaves), 1))
    local_masks = masks(2 * leaves, lambda r: r)

    def turned(ref, chosen):
        parts = split(ref[...])
        return tuple(nt(chosen, part).astype(BF16) for part in parts)

    edges, links = (eh_ref, el_ref), (vh_ref, vl_ref)
    local_blocks = 2 * leaves // NODES
    member_blocks = max(1, 2 * members // NODES)
    group_blocks = max(1, 2 * groups // NODES)

    def reader(refs, base):
        return lambda first, count: rows_of(refs, base + first, count)

    local_e, local_v = reader(edges, 0), reader(links, 0)
    member_e, member_v = reader(edges, local_blocks), reader(links, local_blocks)
    group_base = local_blocks + member_blocks
    group_e, group_v = reader(edges, group_base), reader(links, group_base)

    loaded(0, le_ref)
    loaded(1, basis_ref)
    loaded(2, own_points)
    operators(turned(le_ref, eye), local_masks[0], edges, 0, spread)
    width = NODES * leaf_points
    leaf_blocks = leaves // NODES
    keep = iota((NODES, width), 0) == iota((NODES, width), 1) // leaf_points
    for j in range(leaf_blocks):
        part = basis_ref[:, j * width : (j + 1) * width].astype(F32)
        for k in range(0, RANK, 2):
            tiles = [
                jnp.where(keep, jnp.broadcast_to(part[k + s : k + s + 1], (NODES, width)), 0.0)
                for s in range(2)
            ]
            basis_blocks[j, k * NODES : (k + 2) * NODES, :] = jnp.concatenate(tiles, axis=0).astype(BF16)
    across = []
    for j in range(leaf_blocks):
        x_part = x_ref[:, halo + j * width : halo + (j + 1) * width]
        across.append(nt(x_part, basis_blocks[j]))
    top = paths(NODES, local_e)[0]
    halves = [
        three(nn, split(side_by_side([across[2 * i], across[2 * i + 1]])), local_e(leaf_blocks + 2 * i, 2))
        for i in range(leaf_blocks // 2)
    ]
    eighth = three(nn, split(side_by_side(halves)), local_e(2, 2))
    device_sum = three(nt, split(top), split(eighth))
    top_ref[...] = top
    for i, block in enumerate([eighth] + halves + across):
        ups_ref[:, i * LANES : (i + 1) * LANES] = block
    own_member = members_ref.at[pl.ds(member * HALF, HALF)]
    own_member[...] = side_by_side([device_sum[:HALF], device_sum[HALF:]])

    def copy_to(src, dst, sent, arrived, peer):
        return pltpu.make_async_remote_copy(
            src_ref=src,
            dst_ref=dst,
            send_sem=sent,
            recv_sem=arrived,
            device_id=peer,
            device_id_type=MESH,
        )

    def member_copy(j):
        return copy_to(own_member, own_member, member_send, member_sem, member_at(j))

    own_group = groups_ref.at[pl.ds(group * HALF, HALF)]

    def group_copy(j):
        return copy_to(own_group, own_group, group_send, group_sem, group_at(j))

    def stand_in_copy(j):
        return copy_to(own_group, own_group, stand_in_send, group_sem, (lat, j * members))

    def all_members():
        part = members_ref.at[0 : (members - 1) * HALF]
        return copy_to(part, part, member_send, member_sem, member_at(member_by(0)))

    def all_groups(sent):
        part = groups_ref.at[0 : (groups - 1) * HALF]
        return copy_to(part, part, sent, group_sem, group_at(group_by(0)))

    own_sums = ext_ref.at[leaves : 2 * leaves]
    first_halo, last_halo = x_ref.at[:, halo : 2 * halo], x_ref.at[:, points : points + halo]
    left_halo, right_halo = x_ref.at[:, 0:halo], x_ref.at[:, halo + points : points + 2 * halo]
    below_sums, above_sums = ext_ref.at[0:leaves], ext_ref.at[2 * leaves : 3 * leaves]
    to_after = copy_to(last_halo, left_halo, side_send.at[0], side_sem.at[0], after_at)
    to_before = copy_to(first_halo, right_halo, side_send.at[1], side_sem.at[1], before_at)
    to_above = copy_to(own_sums, below_sums, side_send.at[2], side_sem.at[2], above_at)
    to_below = copy_to(own_sums, above_sums, side_send.at[3], side_sem.at[3], below_at)
    from_before, from_after, from_below, from_above = to_after, to_before, to_above, to_below
    side_copies = [to_after, to_before, to_above, to_below]

    each(members, lambda t: t < member_turn, lambda t: member_copy(member_by(t)).start())
    for k in range(2):
        pl.when(earlier[k])(side_copies[k].start)

    for j in range(leaf_blocks):
        x_part = x_ref[:, halo + j * width : halo + (j + 1) * width]
        by_rank = nt(basis_blocks[j], x_part)
        for k in range(RANK // 2):
            ext_ref[leaves + j * NODES : leaves + (j + 1) * NODES, k * LANES : (k + 1) * LANES] = side_by_side(
                [
                    by_rank[k * NODES : (k + 1) * NODES],
                    by_rank[(k + RANK // 2) * NODES : (k + RANK // 2 + 1) * NODES],
                ]
            )

    for k in range(2, 4):
        pl.when(earlier[k])(side_copies[k].start)

    member_slots, group_slots = member_blocks * NODES, group_blocks * NODES
    upper_rows = member_slots + group_slots
    upper_nodes = upper_edge.shape[1]
    slot = iota((upper_rows, upper_nodes), 0)
    scale = jnp.where(slot >= 2, 2, 1)
    for power in range(2, members.bit_length()):
        scale = jnp.where(slot >= 2**power, 2**power, scale)
    wanted = jnp.where(slot < member_slots, slot + (groups + group - 1) * scale, slot - member_slots)
    chosen = one_hot(wanted == iota((upper_rows, upper_nodes), 1))
    upper_masks = masks(upper_rows, lambda r: jnp.where(r < member_slots, r, r - member_slots))
    loaded(3, upper_ref)
    operators(turned(upper_ref.at[0], chosen), upper_masks[0], edges, local_blocks, spread)

    member_order = [stacked(members, half) for half in range(2)]
    member_paths = [split(block) for block in paths(members, member_e)]
    for half in range(2):
        parts = [picked_by(nt, block, member_order[half]) for block in member_paths]
        for i, part in enumerate(split(side_by_side(parts) if len(parts) > 1 else parts[0])):
            to_group_ref[i, half * RANK : (half + 1) * RANK, :] = part

    blank = jnp.zeros((leaf_points, leaf_points), BF16)
    pair_points = 2 * leaf_points
    span = near.shape[2] + leaf_points
    pairs = source.shape[1]
    half = RANK // 2

    def near_part(j, low, high, add):
        first = side_by_side([near_ref[2 * j], blank])
        second = side_by_side([blank, near_ref[2 * j + 1]])
        weights = jnp.concatenate([first, second], axis=0)[:, low:high]
        window = x_ref[:, j * pair_points + low : j * pair_points + high]
        cut = slice(j * pair_points, (j + 1) * pair_points)
        part = nt(window, weights)
        acc_ref[:, cut] = acc_ref[:, cut] + part if add else part

    def maps_work():
        loaded(4, linked_ref)
        operators(turned(upper_ref.at[1], chosen), upper_masks[1], links, local_blocks, spread)
        operators(turned(linked_ref.at[0], eye), local_masks[1], links, 0, spread)

        own_rows, own_lanes = iota((RANK, LANES), 0), iota((RANK, LANES), 1)
        starts = []
        for i in range(len(member_paths)):
            mine = member - i * NODES if members >= NODES else member + members
            inside = (mine >= 0) & (mine < NODES)
            starts.append(jnp.where((own_lanes == own_rows * NODES + mine) & inside, 1.0, 0.0))
        member_ups = climb(starts, members, member_e)
        group_slot = group if groups >= NODES else group + groups
        place = one_hot((row // NODES == lane // NODES) & (row % NODES == 1) & (lane % NODES == group_slot))
        placed = picked_by(nn, split(three(nn, split(member_ups[0]), member_e(0, 1))), place)
        group_ups = climb([placed], groups, group_e)
        trees = [
            (descend(member_ups, members, member_e, member_v, nn), members),
            (descend(group_ups, groups, group_e, group_v, nn), groups),
        ]
        maps = []
        for blocks, count in trees:
            parts = [split(block) for block in blocks]
            maps += [picked_by(nt, part, stacked(count, half)) for half in range(2) for part in parts]
        for i, part in enumerate(split(side_by_side(maps))):
            map_ref[i] = jnp.concatenate([part] * 3, axis=0)

    def local_work():
        local_ups = {i + 1: ups_ref[:, i * LANES : (i + 1) * LANES] for i in range(2 * leaf_blocks - 1)}
        for j, block in enumerate(descend(crown(local_ups, local_e), leaves, local_e, local_v, nt)):
            local_down_ref[:, j * LANES : (j + 1) * LANES] = block
        for j, block in enumerate(longer([top_ref[...]], leaves, local_e)):
            folded = split(picked_by(nn, split(block), basis_blocks[j]))
            cut = slice(j * width, (j + 1) * width)
            final_ref[0:RANK, cut] = folded[0]
            final_ref[RANK : 2 * RANK, cut] = folded[0]
            final_ref[2 * RANK : 3 * RANK, cut] = folded[1]

        loaded(6, near_ref)
        for j in range(leaves // 2):
            low, high = (halo if j == 0 else 0), (span - halo if j == leaves // 2 - 1 else span)
            near_part(j, low, high, False)

        loaded(5, pairs_ref)
        wide_target = side_by_side([pairs_ref[1], pairs_ref[1]])
        hits = jnp.where(iota((leaves, 2 * pairs), 0) == wide_target, 1.0, 0.0)
        link_rows = linked_ref[1].reshape(RANK, 2, half, pairs)
        link_rows = jnp.concatenate([link_rows[:, 0], link_rows[:, 1]], axis=2)
        link_high = link_rows.astype(BF16).astype(F32)
        for ref, part in ((pair_high_ref, link_high), (pair_low_ref, link_rows - link_high)):
            for j in range(leaf_blocks):
                hit = hits[j * NODES : (j + 1) * NODES]
                for k in range(half):
                    ref[j * LANES : (j + 1) * LANES, k * LANES : (k + 1) * LANES] = jnp.concatenate(
                        [hit * part[a, k : k + 1] for a in range(RANK)], axis=0
                    ).astype(BF16)

    wait(side_in, jnp.where(later[0], 1, 0) + jnp.where(later[2], 1, 0))
    for k in (0, 2):
        pl.when(later[k])(side_copies[k].start)

    def late_sends():
        last = members - member_shift
        wait(member_in, last - 1 - member_turn)
        each(members, lambda t: (t > member_turn) & (t < last), lambda t: member_copy(member_by(t)).start())

    def beside():
        by_last = (member_shift == 1) & (flat > 0)

        @pl.when(by_last | later[3])
        def _():
            pl.semaphore_wait(last_in, 1)

        @pl.when(by_last)
        def _():
            member_copy(0).start()

        for k in (1, 3):
            pl.when(later[k])(side_copies[k].start)

        pl.when(below)(from_below.wait_recv)
        pl.when(above)(from_above.wait_recv)

        @pl.when(jnp.logical_not(below))
        def _():
            below_sums[...] = jnp.zeros(below_sums.shape, F32)

        @pl.when(jnp.logical_not(above))
        def _():
            above_sums[...] = jnp.zeros(above_sums.shape, F32)

        spot = iota((3 * leaves, pairs), 0)
        reads = jnp.where(spot == pairs_ref[0], 1.0, 0.0)
        reads = jnp.transpose(reads).astype(BF16)
        found = [nn(reads, part) for part in split(ext_ref[...])]
        left_side = iota((pairs, LANES), 1) < vectors
        rights = []
        for k in range(half):
            high, low = (part[:, k * LANES : (k + 1) * LANES] for part in found)
            rights.append(jnp.where(left_side, high, pltpu.roll(low, vectors, 1)))
            rights.append(jnp.where(left_side, pltpu.roll(high, vectors, 1), low))
        rights = jnp.concatenate(rights, axis=0).astype(BF16)
        for j in range(leaf_blocks):
            block = slice(j * LANES, (j + 1) * LANES)
            high_both = nn(pair_high_ref[block, :], rights)
            added = high_both[:, :vectors] + (high_both[:, vectors:] + nn(pair_low_ref[block, :], rights[:, :vectors]))
            down = local_down_ref[:, block] + jnp.transpose(added)
            cut = slice(j * width, (j + 1) * width)
            acc_ref[:, cut] = acc_ref[:, cut] + picked_by(nn, split(down), basis_blocks[j])

        pl.when(before)(from_before.wait_recv)
        pl.when(after)(from_after.wait_recv)

        @pl.when(jnp.logical_not(before))
        def _():
            left_halo[...] = jnp.zeros((vectors, halo), BF16)

        @pl.when(jnp.logical_not(after))
        def _():
            right_halo[...] = jnp.zeros((vectors, halo), BF16)

        near_part(0, 0, halo, True)
        near_part(leaves // 2 - 1, span - halo, span, True)

    def relay():
        all_members().wait_recv()
        both = three(nn, (to_group_ref[0], to_group_ref[1]), split(members_ref[...]))
        group_sum = both[:RANK, :vectors] + both[RANK:, vectors:]
        own_group[...] = side_by_side([group_sum[:HALF], group_sum[HALF:]])

        @pl.when(flat > 0)
        def _():
            each(groups, lambda t: t < group_turn, lambda t: group_copy(group_by(t)).start())

        wait(group_in, groups - 1 - group_turn)
        each(groups, lambda t: t > group_turn, lambda t: group_copy(group_by(t)).start())

        @pl.when(stand_in)
        def _():
            for j in range(1, groups):
                stand_in_copy(j).start()

    maps_work()
    late_sends()

    def stage(step, carry):
        turn = jnp.where((member_shift == 1) | (step == 0), step, 3 - step)
        pl.when(turn == 0)(local_work)
        pl.when(turn == 1)(beside)
        pl.when(turn == 2)(relay)
        return carry

    lax.fori_loop(0, 3, stage, 0)

    def mapped(ref, first, count):
        turned_sums = jnp.transpose(ref[...])
        turned_sums = split(side_by_side([turned_sums[:vectors], turned_sums[vectors:]]))
        cut = slice(first * RANK, (first + count) * RANK)
        return three(nt, turned_sums, (map_ref[0][:, cut], map_ref[1][:, cut]))

    here_ref[...] = mapped(members_ref, 0, members)
    all_groups(group_send).wait_recv()
    down_here = here_ref[...] + mapped(groups_ref, members, groups)
    down_parts = split(down_here)
    lanes3 = iota(down_here.shape, 1)
    middle = (lanes3 >= RANK) & (lanes3 < 2 * RANK)
    down3 = jnp.where(middle, down_parts[1].astype(F32), down_parts[0].astype(F32))
    down_ref[...] = down3.astype(BF16)

    all_members().wait_send()
    pl.when(flat > 0)(all_groups(group_send).wait_send)
    pl.when(stand_in)(all_groups(stand_in_send).wait_send)
    pl.when(after)(to_after.wait_send)
    pl.when(before)(to_before.wait_send)
    pl.when(above)(to_above.wait_send)
    pl.when(below)(to_below.wait_send)


def last_part(acc_ref, final_ref, down_ref, out_ref, held_ref, sem):
    down3 = down_ref[...]
    points = out_ref.shape[1]
    width = points // 4
    for j in range(4):
        cut = slice(j * width, (j + 1) * width)
        held_ref[:, cut] = acc_ref[:, cut] + nn(down3, final_ref[:, cut])
        pltpu.make_async_copy(held_ref.at[:, cut], out_ref.at[:, cut], sem).start()
    pltpu.make_async_copy(held_ref, out_ref, sem).wait()


def split_lon(n_lon):
    members = 16 if n_lon >= 128 else 1 << n_lon.bit_length() // 2
    return n_lon // members, members


def shards(
    n_lat,
    n_lon,
    ensemble,
    leaf_basis,
    near_blocks,
    local_transfer,
    local_coupling,
    upper_transfer,
    upper_coupling,
    pair_source,
    pair_target,
    pair_coupling,
):
    vectors, points = ensemble.shape
    leaves, leaf_points, window = near_blocks.shape
    halo = window // 2 - leaf_points // 2
    groups, members = split_lon(n_lon)
    pairs = pair_source.shape[2]

    def by_node(matrices):
        nodes = matrices.shape[1]
        return jnp.transpose(matrices[0], (1, 2, 0)).reshape(RANK * RANK, nodes)

    member_blocks = max(1, 2 * members // NODES)
    group_blocks = max(1, 2 * groups // NODES)
    blocks = 2 * leaves // NODES + member_blocks + group_blocks
    upper_nodes = upper_transfer.shape[1]
    operands = (
        ensemble,
        leaf_basis,
        near_blocks,
        by_node(local_transfer),
        by_node(local_coupling),
        by_node(upper_transfer),
        by_node(upper_coupling),
        pair_source[0],
        pair_target[0],
        by_node(pair_coupling[0]),
    )
    scratch = [
        ((vectors, points + 2 * halo), BF16),
        ((RANK, points), BF16),
        (near_blocks.shape, BF16),
        ((RANK * RANK, 2 * leaves), F32),
        ((2, RANK * RANK, 2 * leaves), F32),
        ((2, RANK * RANK, upper_nodes), F32),
        ((2, 1, pairs), jnp.int32),
        ((blocks * LANES, LANES), BF16),
        ((blocks * LANES, LANES), BF16),
        ((blocks * LANES, LANES), BF16),
        ((blocks * LANES, LANES), BF16),
        ((leaves // NODES, LANES, NODES * leaf_points), BF16),
        ((vectors, (2 * leaves // NODES - 1) * LANES), F32),
        ((RANK, LANES), F32),
        ((3 * leaves, RANK * vectors), F32),
        ((members * HALF, LANES), F32),
        ((groups * HALF, LANES), F32),
        ((2, 2 * RANK, members * HALF), BF16),
        ((2, 3 * RANK, (members + groups) * RANK), BF16),
        ((vectors, leaves * RANK), F32),
        ((leaves * RANK, 2 * pairs * RANK // 2), BF16),
        ((leaves * RANK, 2 * pairs * RANK // 2), BF16),
        ((vectors, 3 * RANK), F32),
    ]
    whole = pl.BlockSpec(memory_space=pltpu.VMEM)
    kept = pl.pallas_call(
        functools.partial(kernel, (n_lat, groups, members)),
        out_shape=(
            jax.ShapeDtypeStruct((vectors, points), F32),
            jax.ShapeDtypeStruct((3 * RANK, points), BF16),
            jax.ShapeDtypeStruct((vectors, 3 * RANK), BF16),
        ),
        in_specs=[pl.BlockSpec(memory_space=pltpu.HBM)] * len(operands),
        out_specs=(whole, whole, whole),
        scratch_shapes=[pltpu.VMEM(shape, dtype) for shape, dtype in scratch]
        + [
            pltpu.SemaphoreType.DMA((7,)),
            pltpu.SemaphoreType.DMA,
            pltpu.SemaphoreType.DMA,
            pltpu.SemaphoreType.DMA,
            pltpu.SemaphoreType.DMA((4,)),
            pltpu.SemaphoreType.DMA,
            pltpu.SemaphoreType.DMA,
            pltpu.SemaphoreType.DMA((4,)),
            pltpu.SemaphoreType.REGULAR,
            pltpu.SemaphoreType.REGULAR,
            pltpu.SemaphoreType.REGULAR,
            pltpu.SemaphoreType.REGULAR,
        ],
        compiler_params=pltpu.CompilerParams(
            collective_id=0, has_side_effects=True, vmem_limit_bytes=40 * 2**20
        ),
        name="h2_tree",
    )(*[pltpu.with_memory_space_constraint(operand, pltpu.HBM) for operand in operands])
    return pl.pallas_call(
        last_part,
        out_shape=jax.ShapeDtypeStruct((vectors, points), F32),
        in_specs=[whole] * 3,
        out_specs=pl.BlockSpec(memory_space=pltpu.HBM),
        scratch_shapes=[pltpu.VMEM((vectors, points), F32), pltpu.SemaphoreType.DMA],
        compiler_params=pltpu.CompilerParams(vmem_limit_bytes=8 * 2**20),
        name="h2_last",
    )(*kept)


def solution(mesh):
    return jax.shard_map(
        functools.partial(shards, mesh.shape["lat"], mesh.shape["lon"]),
        mesh=mesh,
        in_specs=(
            P(None, ("lat", "lon")),
            P(None, ("lat", "lon")),
            P(("lat", "lon"), None, None),
            P(("lat", "lon"), None, None, None),
            P(("lat", "lon"), None, None, None),
            P("lat", None, None, None),
            P("lat", None, None, None),
            P("lat", "lon", None),
            P("lat", "lon", None),
            P("lat", "lon", None, None, None),
        ),
        out_specs=P(None, ("lat", "lon")),
        check_vma=False,
    )
```

```python
import functools

import jax
import jax.numpy as jnp
from jax import lax
from jax.experimental import pallas as pl
from jax.experimental.pallas import tpu as pltpu
from jax.sharding import PartitionSpec as P

F32 = jnp.float32
BF16 = jnp.bfloat16
RANK = 16
LANES = 128
HALF = RANK // 2
NODES = 8
MESH = pl.DeviceIdType.MESH


def iota(shape, axis):
    return lax.broadcasted_iota(jnp.int32, shape, axis)


def one_hot(mask):
    return jnp.where(mask, 1.0, 0.0).astype(BF16)


def nn(a, b):
    return lax.dot_general(a, b, (((1,), (0,)), ((), ())), preferred_element_type=F32)


def nt(a, b):
    return lax.dot_general(a, b, (((1,), (1,)), ((), ())), preferred_element_type=F32)


def split(x):
    high = x.astype(BF16)
    return high, (x - high.astype(F32)).astype(BF16)


def three(dot, a, b):
    rows = a[0].shape[0]
    both = dot(jnp.concatenate(a, axis=0), b[0])
    return both[:rows] + (both[rows:] + dot(a[0], b[1]))


def picked_by(dot, a, b):
    rows = a[0].shape[0]
    both = dot(jnp.concatenate(a, axis=0), b)
    return both[:rows] + both[rows:]


def picks(dot, a, b):
    return dot(a, b[0]) + dot(a, b[1])


def side_by_side(parts):
    return jnp.concatenate(parts, axis=1)


def rows_of(refs, first, count):
    return tuple(ref[pl.ds(first * LANES, count * LANES), :] for ref in refs)


def each(count, wanted, act):
    for turn in range(count):
        pl.when(wanted(turn))(functools.partial(act, turn))


def wait(semaphore, count):
    pl.when(count > 0)(lambda: pl.semaphore_wait(semaphore, count))


def turn_of(index, count):
    return jnp.where(index <= count // 2, jnp.maximum(2 * index - 1, 0), 2 * (count - index))


def index_at(turn, count):
    return jnp.where(turn % 2 == 1, (turn + 1) // 2, jnp.where(turn == 0, 0, count - turn // 2))


def climb(leaves, count, edge):
    ups = {}
    if count < NODES:
        ups[0] = leaves[0]
        if count >= 4:
            ups[0] = ups[0] + three(nn, split(ups[0]), edge(0, 1))
        return ups
    level = count // NODES
    for i, block in enumerate(leaves):
        ups[level + i] = block
    while level > 1:
        for i in range(level // 2, level):
            pair = side_by_side([ups[2 * i], ups[2 * i + 1]])
            ups[i] = three(nn, split(pair), edge(2 * i, 2))
        level //= 2
    return crown(ups, edge)


def crown(ups, edge):
    ups[0] = three(nn, split(ups[1]), edge(1, 1))
    ups[0] = ups[0] + three(nn, split(ups[0]), edge(0, 1))
    return ups


def descend(ups, count, edge, link, across):
    rows = ups[0].shape[0]
    top = three(across, split(ups[0]), link(0, 1))
    if count >= 4:
        slot = iota((rows, LANES), 1) % NODES
        first = jnp.where((slot == 2) | (slot == 3), top, 0.0)
        top = top + three(nt, split(first), edge(0, 1))
    if count < NODES:
        return [top]
    level = [three(across, split(ups[1]), link(1, 1)) + three(nt, split(top), edge(1, 1))]
    while len(level) < count // NODES:
        width = len(level)
        below = []
        for i, block in enumerate(level):
            node = width + i
            both = three(nt, split(block), edge(2 * node, 2))
            for side in range(2):
                child = 2 * node + side
                own = three(across, split(ups[child]), link(child, 1))
                below.append(own + both[:, side * LANES : (side + 1) * LANES])
        level = below
    return level


def paths(count, edge):
    start = one_hot(iota((RANK, LANES), 1) == iota((RANK, LANES), 0) * NODES + 1)
    step = picks(nt, start, edge(0, 1))
    if count >= 4:
        step = three(nt, split(step), edge(0, 1))
    if count < NODES:
        return [step]
    return longer([three(nt, split(step), edge(1, 1))], count, edge)


def longer(level, count, edge):
    while len(level) < count // NODES:
        below = []
        for i, block in enumerate(level):
            both = three(nt, split(block), edge(2 * (len(level) + i), 2))
            below += [both[:, :LANES], both[:, LANES:]]
        level = below
    return level


def stacked(count, half):
    members = min(count, NODES)
    offset = count if count < NODES else 0
    row = iota((members * HALF, LANES), 0)
    lane = iota((members * HALF, LANES), 1)
    return one_hot(lane == (half * HALF + row % HALF) * NODES + row // HALF + offset)


def operators(turned, masks, edge_refs, block, spread):
    (high, low), mask = turned, masks
    nodes = high.shape[0]
    for half in range(2):
        cut = slice(half * LANES, (half + 1) * LANES)
        both = jnp.concatenate([high[:, cut], low[:, cut]], axis=0)
        for pair in range(NODES // 2):
            wide = nn(both, spread[pair])
            parts = [
                [
                    jnp.where(mask, wide[k * nodes : (k + 1) * nodes, s * LANES : (s + 1) * LANES], 0.0)
                    for s in range(2)
                ]
                for k in range(2)
            ]
            for k in range(2):
                for j in range(nodes // NODES):
                    rows = slice(j * NODES, (j + 1) * NODES)
                    tile = jnp.concatenate([parts[k][0][rows], parts[k][1][rows]], axis=0)
                    start = (block + j) * LANES + (half * NODES + 2 * pair) * NODES
                    edge_refs[k][start : start + 2 * NODES, :] = tile.astype(BF16)


def kernel(
    sizes,
    ensemble,
    basis,
    near,
    local_edge,
    local_link,
    upper_edge,
    upper_link,
    source,
    target,
    pair_link,
    acc_ref,
    final_ref,
    down_ref,
    x_ref,
    basis_ref,
    near_ref,
    le_ref,
    linked_ref,
    upper_ref,
    pairs_ref,
    eh_ref,
    el_ref,
    vh_ref,
    vl_ref,
    basis_blocks,
    ups_ref,
    top_ref,
    ext_ref,
    members_ref,
    groups_ref,
    to_group_ref,
    map_ref,
    local_down_ref,
    pair_high_ref,
    pair_low_ref,
    here_ref,
    load_sem,
    member_send,
    group_send,
    stand_in_send,
    side_send,
    member_sem,
    group_sem,
    side_sem,
    member_in,
    group_in,
    side_in,
    last_in,
):
    n_lat, groups, members = sizes
    n_lon = groups * members
    vectors, points = ensemble.shape
    leaves = near.shape[0]
    leaf_points = near.shape[1]
    halo = near.shape[2] // 2 - leaf_points // 2
    lat, lon = lax.axis_index("lat"), lax.axis_index("lon")
    group, member = lon // members, lax.rem(lon, members)
    flat = lat * n_lon + lon
    total = n_lat * n_lon

    member_shift = jnp.where((lat == 0) & (group == 0), 1, 0)
    group_shift = jnp.where((lat == 0) & (member == 0), 1, 0)
    cores = min(members, 2)
    lines = members // cores
    member_turn = turn_of(member // cores, lines) * cores + lax.rem(member, cores)
    member_turn = lax.rem(member_turn + members - member_shift, members)
    group_turn = lax.rem(turn_of(group, groups) + groups - group_shift, groups)

    def member_by(turn):
        turn = lax.rem(turn + member_shift, members)
        return index_at(turn // cores, lines) * cores + lax.rem(turn, cores)

    def group_by(turn):
        return index_at(lax.rem(turn + group_shift, groups), groups)

    def member_at(j):
        return (lat, group * members + j)

    def group_at(j):
        return (lat, j * members + member)

    after, before = flat < total - 1, flat > 0
    above, below = lat < n_lat - 1, lat > 0
    after_at = ((flat + 1) // n_lon, lax.rem(flat + 1, n_lon))
    before_at = ((flat - 1) // n_lon, lax.rem(flat + total - 1, n_lon))
    above_at, below_at = (lat + 1, lon), (lat - 1, lon)
    earlier = [after & (flat == 0), before & (flat != 1), above & (flat == 0), below & (flat != n_lon)]
    later = [after & (flat != 0), before & (flat == 1), above & (flat != 0), below & (flat == n_lon)]
    beside_at = [after_at, before_at, above_at, below_at]
    mirror = [1, 0, 3, 2]

    own_points = x_ref.at[:, halo : halo + points]
    sources = [
        (0, local_edge, le_ref),
        (1, basis, basis_ref),
        (2, ensemble, own_points),
        (3, upper_edge, upper_ref.at[0]),
        (3, upper_link, upper_ref.at[1]),
        (4, local_link, linked_ref.at[0]),
        (4, pair_link, linked_ref.at[1]),
        (5, source, pairs_ref.at[0]),
        (5, target, pairs_ref.at[1]),
        (6, near, near_ref),
    ]
    def load(some):
        for i, src, dst in some:
            pltpu.make_async_copy(src, dst, load_sem.at[i]).start()

    load(sources[:3])

    def loaded(i, ref):
        pltpu.make_async_copy(ref, ref, load_sem.at[i]).wait()

    barrier = pltpu.get_barrier_semaphore()

    def signal(semaphore, peer):
        pl.semaphore_signal(semaphore, inc=1, device_id=peer, device_id_type=MESH)

    each(members, lambda t: t > member_turn, lambda t: signal(barrier, member_at(member_by(t))))
    each(groups, lambda t: t > group_turn, lambda t: signal(barrier, group_at(group_by(t))))
    for there, peer in zip(later, beside_at):
        pl.when(there)(functools.partial(signal, barrier, peer))
    stand_in = flat == 1
    stood_for = (lat == 0) & (member == 0) & (group > 0)
    pl.when(stood_for)(lambda: signal(barrier, (lat, 1)))

    heard = member_turn + group_turn + jnp.where(stand_in, groups - 1, 0)
    for there in earlier:
        heard = heard + jnp.where(there, 1, 0)
    wait(barrier, heard)
    is_last = flat == 0

    @pl.when(is_last)
    def _():
        for j in range(1, members):
            signal(last_in, member_at(j))
        pl.when(above)(lambda: signal(last_in, above_at))

    @pl.when(flat > 0)
    def _():
        each(members, lambda t: t < member_turn, lambda t: signal(member_in, member_at(member_by(t))))
        for k in range(4):
            pl.when(earlier[k])(functools.partial(signal, side_in, beside_at[k]))

    each(groups, lambda t: t < group_turn, lambda t: signal(group_in, group_at(group_by(t))))

    load(sources[3:])

    row, lane = iota((LANES, LANES), 0), iota((LANES, LANES), 1)
    offset = row - lane // NODES
    spread = []
    for pair in range(NODES // 2):
        spread.append(
            side_by_side([one_hot(offset == (2 * pair + s) * RANK) for s in range(2)])
        )

    def masks(count, slots):
        node_slot = slots(iota((count, LANES), 0))
        column = iota((count, LANES), 1) % NODES
        inner = node_slot >= 2
        edge = inner & (column == (node_slot // 2) % NODES)
        link = inner & (column == (node_slot + 1 - 2 * (node_slot % 2)) % NODES)
        return edge, link

    eye = one_hot(iota((2 * leaves, 2 * leaves), 0) == iota((2 * leaves, 2 * leaves), 1))
    local_masks = masks(2 * leaves, lambda r: r)

    def turned(ref, chosen):
        parts = split(ref[...])
        return tuple(nt(chosen, part).astype(BF16) for part in parts)

    edges, links = (eh_ref, el_ref), (vh_ref, vl_ref)
    local_blocks = 2 * leaves // NODES
    member_blocks = max(1, 2 * members // NODES)
    group_blocks = max(1, 2 * groups // NODES)

    def reader(refs, base):
        return lambda first, count: rows_of(refs, base + first, count)

    local_e, local_v = reader(edges, 0), reader(links, 0)
    member_e, member_v = reader(edges, local_blocks), reader(links, local_blocks)
    group_base = local_blocks + member_blocks
    group_e, group_v = reader(edges, group_base), reader(links, group_base)

    loaded(0, le_ref)
    loaded(1, basis_ref)
    loaded(2, own_points)
    operators(turned(le_ref, eye), local_masks[0], edges, 0, spread)
    width = NODES * leaf_points
    leaf_blocks = leaves // NODES
    keep = iota((NODES, width), 0) == iota((NODES, width), 1) // leaf_points
    for j in range(leaf_blocks):
        part = basis_ref[:, j * width : (j + 1) * width].astype(F32)
        for k in range(0, RANK, 2):
            tiles = [
                jnp.where(keep, jnp.broadcast_to(part[k + s : k + s + 1], (NODES, width)), 0.0)
                for s in range(2)
            ]
            basis_blocks[j, k * NODES : (k + 2) * NODES, :] = jnp.concatenate(tiles, axis=0).astype(BF16)
    across = []
    for j in range(leaf_blocks):
        x_part = x_ref[:, halo + j * width : halo + (j + 1) * width]
        across.append(nt(x_part, basis_blocks[j]))
    top = paths(NODES, local_e)[0]
    halves = [
        three(nn, split(side_by_side([across[2 * i], across[2 * i + 1]])), local_e(leaf_blocks + 2 * i, 2))
        for i in range(leaf_blocks // 2)
    ]
    eighth = three(nn, split(side_by_side(halves)), local_e(2, 2))
    device_sum = three(nt, split(top), split(eighth))
    top_ref[...] = top
    for i, block in enumerate([eighth] + halves + across):
        ups_ref[:, i * LANES : (i + 1) * LANES] = block
    own_member = members_ref.at[pl.ds(member * HALF, HALF)]
    own_member[...] = side_by_side([device_sum[:HALF], device_sum[HALF:]])

    def copy_to(src, dst, sent, arrived, peer):
        return pltpu.make_async_remote_copy(
            src_ref=src,
            dst_ref=dst,
            send_sem=sent,
            recv_sem=arrived,
            device_id=peer,
            device_id_type=MESH,
        )

    def member_copy(j):
        return copy_to(own_member, own_member, member_send, member_sem, member_at(j))

    own_group = groups_ref.at[pl.ds(group * HALF, HALF)]

    def group_copy(j):
        return copy_to(own_group, own_group, group_send, group_sem, group_at(j))

    def stand_in_copy(j):
        return copy_to(own_group, own_group, stand_in_send, group_sem, (lat, j * members))

    def all_members():
        part = members_ref.at[0 : (members - 1) * HALF]
        return copy_to(part, part, member_send, member_sem, member_at(member_by(0)))

    def all_groups(sent):
        part = groups_ref.at[0 : (groups - 1) * HALF]
        return copy_to(part, part, sent, group_sem, group_at(group_by(0)))

    own_sums = ext_ref.at[leaves : 2 * leaves]
    first_halo, last_halo = x_ref.at[:, halo : 2 * halo], x_ref.at[:, points : points + halo]
    left_halo, right_halo = x_ref.at[:, 0:halo], x_ref.at[:, halo + points : points + 2 * halo]
    below_sums, above_sums = ext_ref.at[0:leaves], ext_ref.at[2 * leaves : 3 * leaves]
    to_after = copy_to(last_halo, left_halo, side_send.at[0], side_sem.at[0], after_at)
    to_before = copy_to(first_halo, right_halo, side_send.at[1], side_sem.at[1], before_at)
    to_above = copy_to(own_sums, below_sums, side_send.at[2], side_sem.at[2], above_at)
    to_below = copy_to(own_sums, above_sums, side_send.at[3], side_sem.at[3], below_at)
    from_before, from_after, from_below, from_above = to_after, to_before, to_above, to_below
    side_copies = [to_after, to_before, to_above, to_below]

    each(members, lambda t: t < member_turn, lambda t: member_copy(member_by(t)).start())
    for k in range(2):
        pl.when(earlier[k])(side_copies[k].start)

    for j in range(leaf_blocks):
        x_part = x_ref[:, halo + j * width : halo + (j + 1) * width]
        by_rank = nt(basis_blocks[j], x_part)
        for k in range(RANK // 2):
            ext_ref[leaves + j * NODES : leaves + (j + 1) * NODES, k * LANES : (k + 1) * LANES] = side_by_side(
                [
                    by_rank[k * NODES : (k + 1) * NODES],
                    by_rank[(k + RANK // 2) * NODES : (k + RANK // 2 + 1) * NODES],
                ]
            )

    for k in range(2, 4):
        pl.when(earlier[k])(side_copies[k].start)

    member_slots, group_slots = member_blocks * NODES, group_blocks * NODES
    upper_rows = member_slots + group_slots
    upper_nodes = upper_edge.shape[1]
    slot = iota((upper_rows, upper_nodes), 0)
    scale = jnp.where(slot >= 2, 2, 1)
    for power in range(2, members.bit_length()):
        scale = jnp.where(slot >= 2**power, 2**power, scale)
    wanted = jnp.where(slot < member_slots, slot + (groups + group - 1) * scale, slot - member_slots)
    chosen = one_hot(wanted == iota((upper_rows, upper_nodes), 1))
    upper_masks = masks(upper_rows, lambda r: jnp.where(r < member_slots, r, r - member_slots))
    loaded(3, upper_ref)
    operators(turned(upper_ref.at[0], chosen), upper_masks[0], edges, local_blocks, spread)

    member_order = [stacked(members, half) for half in range(2)]
    member_paths = [split(block) for block in paths(members, member_e)]
    for half in range(2):
        parts = [picked_by(nt, block, member_order[half]) for block in member_paths]
        for i, part in enumerate(split(side_by_side(parts) if len(parts) > 1 else parts[0])):
            to_group_ref[i, half * RANK : (half + 1) * RANK, :] = part

    blank = jnp.zeros((leaf_points, leaf_points), BF16)
    pair_points = 2 * leaf_points
    span = near.shape[2] + leaf_points
    pairs = source.shape[1]
    half = RANK // 2

    def near_part(j, low, high, add):
        first = side_by_side([near_ref[2 * j], blank])
        second = side_by_side([blank, near_ref[2 * j + 1]])
        weights = jnp.concatenate([first, second], axis=0)[:, low:high]
        window = x_ref[:, j * pair_points + low : j * pair_points + high]
        cut = slice(j * pair_points, (j + 1) * pair_points)
        part = nt(window, weights)
        acc_ref[:, cut] = acc_ref[:, cut] + part if add else part

    def maps_work():
        loaded(4, linked_ref)
        operators(turned(upper_ref.at[1], chosen), upper_masks[1], links, local_blocks, spread)
        operators(turned(linked_ref.at[0], eye), local_masks[1], links, 0, spread)

        own_rows, own_lanes = iota((RANK, LANES), 0), iota((RANK, LANES), 1)
        starts = []
        for i in range(len(member_paths)):
            mine = member - i * NODES if members >= NODES else member + members
            inside = (mine >= 0) & (mine < NODES)
            starts.append(jnp.where((own_lanes == own_rows * NODES + mine) & inside, 1.0, 0.0))
        member_ups = climb(starts, members, member_e)
        group_slot = group if groups >= NODES else group + groups
        place = one_hot((row // NODES == lane // NODES) & (row % NODES == 1) & (lane % NODES == group_slot))
        placed = picked_by(nn, split(three(nn, split(member_ups[0]), member_e(0, 1))), place)
        group_ups = climb([placed], groups, group_e)
        trees = [
            (descend(member_ups, members, member_e, member_v, nn), members),
            (descend(group_ups, groups, group_e, group_v, nn), groups),
        ]
        maps = []
        for blocks, count in trees:
            parts = [split(block) for block in blocks]
            maps += [picked_by(nt, part, stacked(count, half)) for half in range(2) for part in parts]
        for i, part in enumerate(split(side_by_side(maps))):
            map_ref[i] = jnp.concatenate([part] * 3, axis=0)

    def local_work():
        local_ups = {i + 1: ups_ref[:, i * LANES : (i + 1) * LANES] for i in range(2 * leaf_blocks - 1)}
        for j, block in enumerate(descend(crown(local_ups, local_e), leaves, local_e, local_v, nt)):
            local_down_ref[:, j * LANES : (j + 1) * LANES] = block
        for j, block in enumerate(longer([top_ref[...]], leaves, local_e)):
            folded = split(picked_by(nn, split(block), basis_blocks[j]))
            cut = slice(j * width, (j + 1) * width)
            final_ref[0:RANK, cut] = folded[0]
            final_ref[RANK : 2 * RANK, cut] = folded[0]
            final_ref[2 * RANK : 3 * RANK, cut] = folded[1]

        loaded(6, near_ref)
        for j in range(leaves // 2):
            low, high = (halo if j == 0 else 0), (span - halo if j == leaves // 2 - 1 else span)
            near_part(j, low, high, False)

        loaded(5, pairs_ref)
        wide_target = side_by_side([pairs_ref[1], pairs_ref[1]])
        hits = jnp.where(iota((leaves, 2 * pairs), 0) == wide_target, 1.0, 0.0)
        link_rows = linked_ref[1].reshape(RANK, 2, half, pairs)
        link_rows = jnp.concatenate([link_rows[:, 0], link_rows[:, 1]], axis=2)
        link_high = link_rows.astype(BF16).astype(F32)
        for ref, part in ((pair_high_ref, link_high), (pair_low_ref, link_rows - link_high)):
            for j in range(leaf_blocks):
                hit = hits[j * NODES : (j + 1) * NODES]
                for k in range(half):
                    ref[j * LANES : (j + 1) * LANES, k * LANES : (k + 1) * LANES] = jnp.concatenate(
                        [hit * part[a, k : k + 1] for a in range(RANK)], axis=0
                    ).astype(BF16)

    wait(side_in, jnp.where(later[0], 1, 0) + jnp.where(later[2], 1, 0))
    for k in (0, 2):
        pl.when(later[k])(side_copies[k].start)

    def late_sends():
        last = members - member_shift
        wait(member_in, last - 1 - member_turn)
        each(members, lambda t: (t > member_turn) & (t < last), lambda t: member_copy(member_by(t)).start())

    def beside():
        by_last = (member_shift == 1) & (flat > 0)

        @pl.when(by_last | later[3])
        def _():
            pl.semaphore_wait(last_in, 1)

        @pl.when(by_last)
        def _():
            member_copy(0).start()

        for k in (1, 3):
            pl.when(later[k])(side_copies[k].start)

        pl.when(below)(from_below.wait_recv)
        pl.when(above)(from_above.wait_recv)

        @pl.when(jnp.logical_not(below))
        def _():
            below_sums[...] = jnp.zeros(below_sums.shape, F32)

        @pl.when(jnp.logical_not(above))
        def _():
            above_sums[...] = jnp.zeros(above_sums.shape, F32)

        spot = iota((3 * leaves, pairs), 0)
        reads = jnp.where(spot == pairs_ref[0], 1.0, 0.0)
        reads = jnp.transpose(reads).astype(BF16)
        found = [nn(reads, part) for part in split(ext_ref[...])]
        left_side = iota((pairs, LANES), 1) < vectors
        rights = []
        for k in range(half):
            high, low = (part[:, k * LANES : (k + 1) * LANES] for part in found)
            rights.append(jnp.where(left_side, high, pltpu.roll(low, vectors, 1)))
            rights.append(jnp.where(left_side, pltpu.roll(high, vectors, 1), low))
        rights = jnp.concatenate(rights, axis=0).astype(BF16)
        for j in range(leaf_blocks):
            block = slice(j * LANES, (j + 1) * LANES)
            high_both = nn(pair_high_ref[block, :], rights)
            added = high_both[:, :vectors] + (high_both[:, vectors:] + nn(pair_low_ref[block, :], rights[:, :vectors]))
            down = local_down_ref[:, block] + jnp.transpose(added)
            cut = slice(j * width, (j + 1) * width)
            acc_ref[:, cut] = acc_ref[:, cut] + picked_by(nn, split(down), basis_blocks[j])

        pl.when(before)(from_before.wait_recv)
        pl.when(after)(from_after.wait_recv)

        @pl.when(jnp.logical_not(before))
        def _():
            left_halo[...] = jnp.zeros((vectors, halo), BF16)

        @pl.when(jnp.logical_not(after))
        def _():
            right_halo[...] = jnp.zeros((vectors, halo), BF16)

        near_part(0, 0, halo, True)
        near_part(leaves // 2 - 1, span - halo, span, True)

    def relay():
        all_members().wait_recv()
        both = three(nn, (to_group_ref[0], to_group_ref[1]), split(members_ref[...]))
        group_sum = both[:RANK, :vectors] + both[RANK:, vectors:]
        own_group[...] = side_by_side([group_sum[:HALF], group_sum[HALF:]])

        @pl.when(flat > 0)
        def _():
            each(groups, lambda t: t < group_turn, lambda t: group_copy(group_by(t)).start())

        wait(group_in, groups - 1 - group_turn)
        each(groups, lambda t: t > group_turn, lambda t: group_copy(group_by(t)).start())

        @pl.when(stand_in)
        def _():
            for j in range(1, groups):
                stand_in_copy(j).start()

    maps_work()
    late_sends()

    def stage(step, carry):
        turn = jnp.where(
            member_shift == 1, step, jnp.where(member < cores, lax.rem(step + 2, 3), jnp.where(step == 0, 0, 3 - step))
        )
        pl.when(turn == 0)(local_work)
        pl.when(turn == 1)(beside)
        pl.when(turn == 2)(relay)
        return carry

    lax.fori_loop(0, 3, stage, 0)

    def mapped(ref, first, count):
        turned_sums = jnp.transpose(ref[...])
        turned_sums = split(side_by_side([turned_sums[:vectors], turned_sums[vectors:]]))
        cut = slice(first * RANK, (first + count) * RANK)
        return three(nt, turned_sums, (map_ref[0][:, cut], map_ref[1][:, cut]))

    here_ref[...] = mapped(members_ref, 0, members)
    all_groups(group_send).wait_recv()
    down_here = here_ref[...] + mapped(groups_ref, members, groups)
    down_parts = split(down_here)
    lanes3 = iota(down_here.shape, 1)
    middle = (lanes3 >= RANK) & (lanes3 < 2 * RANK)
    down3 = jnp.where(middle, down_parts[1].astype(F32), down_parts[0].astype(F32))
    down_ref[...] = down3.astype(BF16)

    all_members().wait_send()
    pl.when(flat > 0)(all_groups(group_send).wait_send)
    pl.when(stand_in)(all_groups(stand_in_send).wait_send)
    pl.when(after)(to_after.wait_send)
    pl.when(before)(to_before.wait_send)
    pl.when(above)(to_above.wait_send)
    pl.when(below)(to_below.wait_send)


def last_part(acc_ref, final_ref, down_ref, out_ref, held_ref, sem):
    down3 = down_ref[...]
    points = out_ref.shape[1]
    width = points // 4
    for j in range(4):
        cut = slice(j * width, (j + 1) * width)
        held_ref[:, cut] = acc_ref[:, cut] + nn(down3, final_ref[:, cut])
        pltpu.make_async_copy(held_ref.at[:, cut], out_ref.at[:, cut], sem).start()
    pltpu.make_async_copy(held_ref, out_ref, sem).wait()


def split_lon(n_lon):
    members = 16 if n_lon >= 128 else 1 << n_lon.bit_length() // 2
    return n_lon // members, members


def shards(
    n_lat,
    n_lon,
    ensemble,
    leaf_basis,
    near_blocks,
    local_transfer,
    local_coupling,
    upper_transfer,
    upper_coupling,
    pair_source,
    pair_target,
    pair_coupling,
):
    vectors, points = ensemble.shape
    leaves, leaf_points, window = near_blocks.shape
    halo = window // 2 - leaf_points // 2
    groups, members = split_lon(n_lon)
    pairs = pair_source.shape[2]

    def by_node(matrices):
        nodes = matrices.shape[1]
        return jnp.transpose(matrices[0], (1, 2, 0)).reshape(RANK * RANK, nodes)

    member_blocks = max(1, 2 * members // NODES)
    group_blocks = max(1, 2 * groups // NODES)
    blocks = 2 * leaves // NODES + member_blocks + group_blocks
    upper_nodes = upper_transfer.shape[1]
    operands = (
        ensemble,
        leaf_basis,
        near_blocks,
        by_node(local_transfer),
        by_node(local_coupling),
        by_node(upper_transfer),
        by_node(upper_coupling),
        pair_source[0],
        pair_target[0],
        by_node(pair_coupling[0]),
    )
    scratch = [
        ((vectors, points + 2 * halo), BF16),
        ((RANK, points), BF16),
        (near_blocks.shape, BF16),
        ((RANK * RANK, 2 * leaves), F32),
        ((2, RANK * RANK, 2 * leaves), F32),
        ((2, RANK * RANK, upper_nodes), F32),
        ((2, 1, pairs), jnp.int32),
        ((blocks * LANES, LANES), BF16),
        ((blocks * LANES, LANES), BF16),
        ((blocks * LANES, LANES), BF16),
        ((blocks * LANES, LANES), BF16),
        ((leaves // NODES, LANES, NODES * leaf_points), BF16),
        ((vectors, (2 * leaves // NODES - 1) * LANES), F32),
        ((RANK, LANES), F32),
        ((3 * leaves, RANK * vectors), F32),
        ((members * HALF, LANES), F32),
        ((groups * HALF, LANES), F32),
        ((2, 2 * RANK, members * HALF), BF16),
        ((2, 3 * RANK, (members + groups) * RANK), BF16),
        ((vectors, leaves * RANK), F32),
        ((leaves * RANK, 2 * pairs * RANK // 2), BF16),
        ((leaves * RANK, 2 * pairs * RANK // 2), BF16),
        ((vectors, 3 * RANK), F32),
    ]
    whole = pl.BlockSpec(memory_space=pltpu.VMEM)
    kept = pl.pallas_call(
        functools.partial(kernel, (n_lat, groups, members)),
        out_shape=(
            jax.ShapeDtypeStruct((vectors, points), F32),
            jax.ShapeDtypeStruct((3 * RANK, points), BF16),
            jax.ShapeDtypeStruct((vectors, 3 * RANK), BF16),
        ),
        in_specs=[pl.BlockSpec(memory_space=pltpu.HBM)] * len(operands),
        out_specs=(whole, whole, whole),
        scratch_shapes=[pltpu.VMEM(shape, dtype) for shape, dtype in scratch]
        + [
            pltpu.SemaphoreType.DMA((7,)),
            pltpu.SemaphoreType.DMA,
            pltpu.SemaphoreType.DMA,
            pltpu.SemaphoreType.DMA,
            pltpu.SemaphoreType.DMA((4,)),
            pltpu.SemaphoreType.DMA,
            pltpu.SemaphoreType.DMA,
            pltpu.SemaphoreType.DMA((4,)),
            pltpu.SemaphoreType.REGULAR,
            pltpu.SemaphoreType.REGULAR,
            pltpu.SemaphoreType.REGULAR,
            pltpu.SemaphoreType.REGULAR,
        ],
        compiler_params=pltpu.CompilerParams(
            collective_id=0, has_side_effects=True, vmem_limit_bytes=40 * 2**20
        ),
        name="h2_tree",
    )(*[pltpu.with_memory_space_constraint(operand, pltpu.HBM) for operand in operands])
    return pl.pallas_call(
        last_part,
        out_shape=jax.ShapeDtypeStruct((vectors, points), F32),
        in_specs=[whole] * 3,
        out_specs=pl.BlockSpec(memory_space=pltpu.HBM),
        scratch_shapes=[pltpu.VMEM((vectors, points), F32), pltpu.SemaphoreType.DMA],
        compiler_params=pltpu.CompilerParams(vmem_limit_bytes=8 * 2**20),
        name="h2_last",
    )(*kept)


def solution(mesh):
    return jax.shard_map(
        functools.partial(shards, mesh.shape["lat"], mesh.shape["lon"]),
        mesh=mesh,
        in_specs=(
            P(None, ("lat", "lon")),
            P(None, ("lat", "lon")),
            P(("lat", "lon"), None, None),
            P(("lat", "lon"), None, None, None),
            P(("lat", "lon"), None, None, None),
            P("lat", None, None, None),
            P("lat", None, None, None),
            P("lat", "lon", None),
            P("lat", "lon", None),
            P("lat", "lon", None, None, None),
        ),
        out_specs=P(None, ("lat", "lon")),
        check_vma=False,
    )
```

```python
import functools

import jax
import jax.numpy as jnp
from jax import lax
from jax.experimental import pallas as pl
from jax.experimental.pallas import tpu as pltpu
from jax.sharding import PartitionSpec as P

F32 = jnp.float32
BF16 = jnp.bfloat16
RANK = 16
LANES = 128
HALF = RANK // 2
NODES = 8
MESH = pl.DeviceIdType.MESH


def iota(shape, axis):
    return lax.broadcasted_iota(jnp.int32, shape, axis)


def one_hot(mask):
    return jnp.where(mask, 1.0, 0.0).astype(BF16)


def nn(a, b):
    return lax.dot_general(a, b, (((1,), (0,)), ((), ())), preferred_element_type=F32)


def nt(a, b):
    return lax.dot_general(a, b, (((1,), (1,)), ((), ())), preferred_element_type=F32)


def split(x):
    high = x.astype(BF16)
    return high, (x - high.astype(F32)).astype(BF16)


def three(dot, a, b):
    rows = a[0].shape[0]
    both = dot(jnp.concatenate(a, axis=0), b[0])
    return both[:rows] + (both[rows:] + dot(a[0], b[1]))


def picked_by(dot, a, b):
    rows = a[0].shape[0]
    both = dot(jnp.concatenate(a, axis=0), b)
    return both[:rows] + both[rows:]


def picks(dot, a, b):
    return dot(a, b[0]) + dot(a, b[1])


def side_by_side(parts):
    return jnp.concatenate(parts, axis=1)


def rows_of(refs, first, count):
    return tuple(ref[pl.ds(first * LANES, count * LANES), :] for ref in refs)


def each(count, wanted, act):
    for turn in range(count):
        pl.when(wanted(turn))(functools.partial(act, turn))


def wait(semaphore, count):
    pl.when(count > 0)(lambda: pl.semaphore_wait(semaphore, count))


def turn_of(index, count):
    return jnp.where(index <= count // 2, jnp.maximum(2 * index - 1, 0), 2 * (count - index))


def index_at(turn, count):
    return jnp.where(turn % 2 == 1, (turn + 1) // 2, jnp.where(turn == 0, 0, count - turn // 2))


def climb(leaves, count, edge):
    ups = {}
    if count < NODES:
        ups[0] = leaves[0]
        if count >= 4:
            ups[0] = ups[0] + three(nn, split(ups[0]), edge(0, 1))
        return ups
    level = count // NODES
    for i, block in enumerate(leaves):
        ups[level + i] = block
    while level > 1:
        for i in range(level // 2, level):
            pair = side_by_side([ups[2 * i], ups[2 * i + 1]])
            ups[i] = three(nn, split(pair), edge(2 * i, 2))
        level //= 2
    return crown(ups, edge)


def crown(ups, edge):
    ups[0] = three(nn, split(ups[1]), edge(1, 1))
    ups[0] = ups[0] + three(nn, split(ups[0]), edge(0, 1))
    return ups


def descend(ups, count, edge, link, across):
    rows = ups[0].shape[0]
    top = three(across, split(ups[0]), link(0, 1))
    if count >= 4:
        slot = iota((rows, LANES), 1) % NODES
        first = jnp.where((slot == 2) | (slot == 3), top, 0.0)
        top = top + three(nt, split(first), edge(0, 1))
    if count < NODES:
        return [top]
    level = [three(across, split(ups[1]), link(1, 1)) + three(nt, split(top), edge(1, 1))]
    while len(level) < count // NODES:
        width = len(level)
        below = []
        for i, block in enumerate(level):
            node = width + i
            both = three(nt, split(block), edge(2 * node, 2))
            for side in range(2):
                child = 2 * node + side
                own = three(across, split(ups[child]), link(child, 1))
                below.append(own + both[:, side * LANES : (side + 1) * LANES])
        level = below
    return level


def paths(count, edge):
    start = one_hot(iota((RANK, LANES), 1) == iota((RANK, LANES), 0) * NODES + 1)
    step = picks(nt, start, edge(0, 1))
    if count >= 4:
        step = three(nt, split(step), edge(0, 1))
    if count < NODES:
        return [step]
    return longer([three(nt, split(step), edge(1, 1))], count, edge)


def longer(level, count, edge):
    while len(level) < count // NODES:
        below = []
        for i, block in enumerate(level):
            both = three(nt, split(block), edge(2 * (len(level) + i), 2))
            below += [both[:, :LANES], both[:, LANES:]]
        level = below
    return level


def stacked(count, half):
    members = min(count, NODES)
    offset = count if count < NODES else 0
    row = iota((members * HALF, LANES), 0)
    lane = iota((members * HALF, LANES), 1)
    return one_hot(lane == (half * HALF + row % HALF) * NODES + row // HALF + offset)


def operators(turned, masks, edge_refs, block, spread):
    (high, low), mask = turned, masks
    nodes = high.shape[0]
    for half in range(2):
        cut = slice(half * LANES, (half + 1) * LANES)
        both = jnp.concatenate([high[:, cut], low[:, cut]], axis=0)
        for pair in range(NODES // 2):
            wide = nn(both, spread[pair])
            parts = [
                [
                    jnp.where(mask, wide[k * nodes : (k + 1) * nodes, s * LANES : (s + 1) * LANES], 0.0)
                    for s in range(2)
                ]
                for k in range(2)
            ]
            for k in range(2):
                for j in range(nodes // NODES):
                    rows = slice(j * NODES, (j + 1) * NODES)
                    tile = jnp.concatenate([parts[k][0][rows], parts[k][1][rows]], axis=0)
                    start = (block + j) * LANES + (half * NODES + 2 * pair) * NODES
                    edge_refs[k][start : start + 2 * NODES, :] = tile.astype(BF16)


def kernel(
    sizes,
    ensemble,
    basis,
    near,
    local_edge,
    local_link,
    upper_edge,
    upper_link,
    source,
    target,
    pair_link,
    acc_ref,
    final_ref,
    down_ref,
    x_ref,
    basis_ref,
    near_ref,
    le_ref,
    linked_ref,
    upper_ref,
    pairs_ref,
    eh_ref,
    el_ref,
    vh_ref,
    vl_ref,
    basis_blocks,
    ups_ref,
    top_ref,
    ext_ref,
    members_ref,
    groups_ref,
    to_group_ref,
    map_ref,
    local_down_ref,
    pair_high_ref,
    pair_low_ref,
    here_ref,
    load_sem,
    member_send,
    group_send,
    stand_in_send,
    side_send,
    member_sem,
    group_sem,
    side_sem,
    member_in,
    group_in,
    side_in,
    last_in,
):
    n_lat, groups, members = sizes
    n_lon = groups * members
    vectors, points = ensemble.shape
    leaves = near.shape[0]
    leaf_points = near.shape[1]
    halo = near.shape[2] // 2 - leaf_points // 2
    lat, lon = lax.axis_index("lat"), lax.axis_index("lon")
    group, member = lon // members, lax.rem(lon, members)
    flat = lat * n_lon + lon
    total = n_lat * n_lon

    member_shift = jnp.where((lat == 0) & (group == 0), 1, 0)
    group_shift = jnp.where((lat == 0) & (member == 0), 1, 0)
    cores = min(members, 2)
    lines = members // cores
    member_turn = turn_of(member // cores, lines) * cores + lax.rem(member, cores)
    member_turn = lax.rem(member_turn + members - member_shift, members)
    group_turn = lax.rem(turn_of(group, groups) + groups - group_shift, groups)

    def member_by(turn):
        turn = lax.rem(turn + member_shift, members)
        return index_at(turn // cores, lines) * cores + lax.rem(turn, cores)

    def group_by(turn):
        return index_at(lax.rem(turn + group_shift, groups), groups)

    def member_at(j):
        return (lat, group * members + j)

    def group_at(j):
        return (lat, j * members + member)

    after, before = flat < total - 1, flat > 0
    above, below = lat < n_lat - 1, lat > 0
    after_at = ((flat + 1) // n_lon, lax.rem(flat + 1, n_lon))
    before_at = ((flat - 1) // n_lon, lax.rem(flat + total - 1, n_lon))
    above_at, below_at = (lat + 1, lon), (lat - 1, lon)
    earlier = [after & (flat == 0), before & (flat != 1), above & (flat == 0), below & (flat != n_lon)]
    later = [after & (flat != 0), before & (flat == 1), above & (flat != 0), below & (flat == n_lon)]
    beside_at = [after_at, before_at, above_at, below_at]
    mirror = [1, 0, 3, 2]

    own_points = x_ref.at[:, halo : halo + points]
    sources = [
        (0, local_edge, le_ref),
        (1, basis, basis_ref),
        (2, ensemble, own_points),
        (3, upper_edge, upper_ref.at[0]),
        (3, upper_link, upper_ref.at[1]),
        (4, local_link, linked_ref.at[0]),
        (4, pair_link, linked_ref.at[1]),
        (5, source, pairs_ref.at[0]),
        (5, target, pairs_ref.at[1]),
        (6, near, near_ref),
    ]
    def load(some):
        for i, src, dst in some:
            pltpu.make_async_copy(src, dst, load_sem.at[i]).start()

    load(sources[:3])

    def loaded(i, ref):
        pltpu.make_async_copy(ref, ref, load_sem.at[i]).wait()

    barrier = pltpu.get_barrier_semaphore()

    def signal(semaphore, peer):
        pl.semaphore_signal(semaphore, inc=1, device_id=peer, device_id_type=MESH)

    each(members, lambda t: t > member_turn, lambda t: signal(barrier, member_at(member_by(t))))
    each(groups, lambda t: t > group_turn, lambda t: signal(barrier, group_at(group_by(t))))
    for there, peer in zip(later, beside_at):
        pl.when(there)(functools.partial(signal, barrier, peer))
    stand_in = flat == 1
    stood_for = (lat == 0) & (member == 0) & (group > 0)
    pl.when(stood_for)(lambda: signal(barrier, (lat, 1)))

    heard = member_turn + group_turn + jnp.where(stand_in, groups - 1, 0)
    for there in earlier:
        heard = heard + jnp.where(there, 1, 0)
    wait(barrier, heard)
    is_last = flat == 0

    @pl.when(is_last)
    def _():
        for j in range(1, members):
            signal(last_in, member_at(j))
        pl.when(above)(lambda: signal(last_in, above_at))

    @pl.when(flat > 0)
    def _():
        each(members, lambda t: t < member_turn, lambda t: signal(member_in, member_at(member_by(t))))
        for k in range(4):
            pl.when(earlier[k])(functools.partial(signal, side_in, beside_at[k]))

    each(groups, lambda t: t < group_turn, lambda t: signal(group_in, group_at(group_by(t))))

    load(sources[3:])

    row, lane = iota((LANES, LANES), 0), iota((LANES, LANES), 1)
    offset = row - lane // NODES
    spread = []
    for pair in range(NODES // 2):
        spread.append(
            side_by_side([one_hot(offset == (2 * pair + s) * RANK) for s in range(2)])
        )

    def masks(count, slots):
        node_slot = slots(iota((count, LANES), 0))
        column = iota((count, LANES), 1) % NODES
        inner = node_slot >= 2
        edge = inner & (column == (node_slot // 2) % NODES)
        link = inner & (column == (node_slot + 1 - 2 * (node_slot % 2)) % NODES)
        return edge, link

    eye = one_hot(iota((2 * leaves, 2 * leaves), 0) == iota((2 * leaves, 2 * leaves), 1))
    local_masks = masks(2 * leaves, lambda r: r)

    def turned(ref, chosen):
        parts = split(ref[...])
        return tuple(nt(chosen, part).astype(BF16) for part in parts)

    edges, links = (eh_ref, el_ref), (vh_ref, vl_ref)
    local_blocks = 2 * leaves // NODES
    member_blocks = max(1, 2 * members // NODES)
    group_blocks = max(1, 2 * groups // NODES)

    def reader(refs, base):
        return lambda first, count: rows_of(refs, base + first, count)

    local_e, local_v = reader(edges, 0), reader(links, 0)
    member_e, member_v = reader(edges, local_blocks), reader(links, local_blocks)
    group_base = local_blocks + member_blocks
    group_e, group_v = reader(edges, group_base), reader(links, group_base)

    loaded(0, le_ref)
    loaded(1, basis_ref)
    loaded(2, own_points)
    operators(turned(le_ref, eye), local_masks[0], edges, 0, spread)
    width = NODES * leaf_points
    leaf_blocks = leaves // NODES
    keep = iota((NODES, width), 0) == iota((NODES, width), 1) // leaf_points
    for j in range(leaf_blocks):
        part = basis_ref[:, j * width : (j + 1) * width].astype(F32)
        for k in range(0, RANK, 2):
            tiles = [
                jnp.where(keep, jnp.broadcast_to(part[k + s : k + s + 1], (NODES, width)), 0.0)
                for s in range(2)
            ]
            basis_blocks[j, k * NODES : (k + 2) * NODES, :] = jnp.concatenate(tiles, axis=0).astype(BF16)
    across = []
    for j in range(leaf_blocks):
        x_part = x_ref[:, halo + j * width : halo + (j + 1) * width]
        across.append(nt(x_part, basis_blocks[j]))
    top = paths(NODES, local_e)[0]
    halves = [
        three(nn, split(side_by_side([across[2 * i], across[2 * i + 1]])), local_e(leaf_blocks + 2 * i, 2))
        for i in range(leaf_blocks // 2)
    ]
    eighth = three(nn, split(side_by_side(halves)), local_e(2, 2))
    device_sum = three(nt, split(top), split(eighth))
    top_ref[...] = top
    for i, block in enumerate([eighth] + halves + across):
        ups_ref[:, i * LANES : (i + 1) * LANES] = block
    own_member = members_ref.at[pl.ds(member * HALF, HALF)]
    own_member[...] = side_by_side([device_sum[:HALF], device_sum[HALF:]])

    def copy_to(src, dst, sent, arrived, peer):
        return pltpu.make_async_remote_copy(
            src_ref=src,
            dst_ref=dst,
            send_sem=sent,
            recv_sem=arrived,
            device_id=peer,
            device_id_type=MESH,
        )

    def member_copy(j):
        return copy_to(own_member, own_member, member_send, member_sem, member_at(j))

    own_group = groups_ref.at[pl.ds(group * HALF, HALF)]

    def group_copy(j):
        return copy_to(own_group, own_group, group_send, group_sem, group_at(j))

    def stand_in_copy(j):
        return copy_to(own_group, own_group, stand_in_send, group_sem, (lat, j * members))

    def all_members():
        part = members_ref.at[0 : (members - 1) * HALF]
        return copy_to(part, part, member_send, member_sem, member_at(member_by(0)))

    def all_groups(sent):
        part = groups_ref.at[0 : (groups - 1) * HALF]
        return copy_to(part, part, sent, group_sem, group_at(group_by(0)))

    own_sums = ext_ref.at[leaves : 2 * leaves]
    first_halo, last_halo = x_ref.at[:, halo : 2 * halo], x_ref.at[:, points : points + halo]
    left_halo, right_halo = x_ref.at[:, 0:halo], x_ref.at[:, halo + points : points + 2 * halo]
    below_sums, above_sums = ext_ref.at[0:leaves], ext_ref.at[2 * leaves : 3 * leaves]
    to_after = copy_to(last_halo, left_halo, side_send.at[0], side_sem.at[0], after_at)
    to_before = copy_to(first_halo, right_halo, side_send.at[1], side_sem.at[1], before_at)
    to_above = copy_to(own_sums, below_sums, side_send.at[2], side_sem.at[2], above_at)
    to_below = copy_to(own_sums, above_sums, side_send.at[3], side_sem.at[3], below_at)
    from_before, from_after, from_below, from_above = to_after, to_before, to_above, to_below
    side_copies = [to_after, to_before, to_above, to_below]

    each(members, lambda t: t < member_turn, lambda t: member_copy(member_by(t)).start())
    for k in range(2):
        pl.when(earlier[k])(side_copies[k].start)

    for j in range(leaf_blocks):
        x_part = x_ref[:, halo + j * width : halo + (j + 1) * width]
        by_rank = nt(basis_blocks[j], x_part)
        for k in range(RANK // 2):
            ext_ref[leaves + j * NODES : leaves + (j + 1) * NODES, k * LANES : (k + 1) * LANES] = side_by_side(
                [
                    by_rank[k * NODES : (k + 1) * NODES],
                    by_rank[(k + RANK // 2) * NODES : (k + RANK // 2 + 1) * NODES],
                ]
            )

    for k in range(2, 4):
        pl.when(earlier[k])(side_copies[k].start)

    member_slots, group_slots = member_blocks * NODES, group_blocks * NODES
    upper_rows = member_slots + group_slots
    upper_nodes = upper_edge.shape[1]
    slot = iota((upper_rows, upper_nodes), 0)
    scale = jnp.where(slot >= 2, 2, 1)
    for power in range(2, members.bit_length()):
        scale = jnp.where(slot >= 2**power, 2**power, scale)
    wanted = jnp.where(slot < member_slots, slot + (groups + group - 1) * scale, slot - member_slots)
    chosen = one_hot(wanted == iota((upper_rows, upper_nodes), 1))
    upper_masks = masks(upper_rows, lambda r: jnp.where(r < member_slots, r, r - member_slots))
    loaded(3, upper_ref)
    operators(turned(upper_ref.at[0], chosen), upper_masks[0], edges, local_blocks, spread)

    member_order = [stacked(members, half) for half in range(2)]
    member_paths = [split(block) for block in paths(members, member_e)]
    for half in range(2):
        parts = [picked_by(nt, block, member_order[half]) for block in member_paths]
        for i, part in enumerate(split(side_by_side(parts) if len(parts) > 1 else parts[0])):
            to_group_ref[i, half * RANK : (half + 1) * RANK, :] = part

    blank = jnp.zeros((leaf_points, leaf_points), BF16)
    pair_points = 2 * leaf_points
    span = near.shape[2] + leaf_points
    pairs = source.shape[1]
    half = RANK // 2

    def near_part(j, low, high, add):
        first = side_by_side([near_ref[2 * j], blank])
        second = side_by_side([blank, near_ref[2 * j + 1]])
        weights = jnp.concatenate([first, second], axis=0)[:, low:high]
        window = x_ref[:, j * pair_points + low : j * pair_points + high]
        cut = slice(j * pair_points, (j + 1) * pair_points)
        part = nt(window, weights)
        acc_ref[:, cut] = acc_ref[:, cut] + part if add else part

    def maps_work():
        loaded(4, linked_ref)
        operators(turned(upper_ref.at[1], chosen), upper_masks[1], links, local_blocks, spread)
        operators(turned(linked_ref.at[0], eye), local_masks[1], links, 0, spread)

        own_rows, own_lanes = iota((RANK, LANES), 0), iota((RANK, LANES), 1)
        starts = []
        for i in range(len(member_paths)):
            mine = member - i * NODES if members >= NODES else member + members
            inside = (mine >= 0) & (mine < NODES)
            starts.append(jnp.where((own_lanes == own_rows * NODES + mine) & inside, 1.0, 0.0))
        member_ups = climb(starts, members, member_e)
        group_slot = group if groups >= NODES else group + groups
        place = one_hot((row // NODES == lane // NODES) & (row % NODES == 1) & (lane % NODES == group_slot))
        placed = picked_by(nn, split(three(nn, split(member_ups[0]), member_e(0, 1))), place)
        group_ups = climb([placed], groups, group_e)
        trees = [
            (descend(member_ups, members, member_e, member_v, nn), members),
            (descend(group_ups, groups, group_e, group_v, nn), groups),
        ]
        maps = []
        for blocks, count in trees:
            parts = [split(block) for block in blocks]
            maps += [picked_by(nt, part, stacked(count, half)) for half in range(2) for part in parts]
        for i, part in enumerate(split(side_by_side(maps))):
            map_ref[i] = jnp.concatenate([part] * 3, axis=0)

    def local_work():
        local_ups = {i + 1: ups_ref[:, i * LANES : (i + 1) * LANES] for i in range(2 * leaf_blocks - 1)}
        for j, block in enumerate(descend(crown(local_ups, local_e), leaves, local_e, local_v, nt)):
            local_down_ref[:, j * LANES : (j + 1) * LANES] = block
        for j, block in enumerate(longer([top_ref[...]], leaves, local_e)):
            folded = split(picked_by(nn, split(block), basis_blocks[j]))
            cut = slice(j * width, (j + 1) * width)
            final_ref[0:RANK, cut] = folded[0]
            final_ref[RANK : 2 * RANK, cut] = folded[0]
            final_ref[2 * RANK : 3 * RANK, cut] = folded[1]

        loaded(6, near_ref)
        for j in range(leaves // 2):
            low, high = (halo if j == 0 else 0), (span - halo if j == leaves // 2 - 1 else span)
            near_part(j, low, high, False)

        loaded(5, pairs_ref)
        wide_target = side_by_side([pairs_ref[1], pairs_ref[1]])
        hits = jnp.where(iota((leaves, 2 * pairs), 0) == wide_target, 1.0, 0.0)
        link_rows = linked_ref[1].reshape(RANK, 2, half, pairs)
        link_rows = jnp.concatenate([link_rows[:, 0], link_rows[:, 1]], axis=2)
        link_high = link_rows.astype(BF16).astype(F32)
        for ref, part in ((pair_high_ref, link_high), (pair_low_ref, link_rows - link_high)):
            for j in range(leaf_blocks):
                hit = hits[j * NODES : (j + 1) * NODES]
                for k in range(half):
                    ref[j * LANES : (j + 1) * LANES, k * LANES : (k + 1) * LANES] = jnp.concatenate(
                        [hit * part[a, k : k + 1] for a in range(RANK)], axis=0
                    ).astype(BF16)

    wait(side_in, jnp.where(later[0], 1, 0) + jnp.where(later[2], 1, 0))
    for k in (0, 2):
        pl.when(later[k])(side_copies[k].start)

    def late_sends():
        last = members - member_shift
        wait(member_in, last - 1 - member_turn)
        each(members, lambda t: (t > member_turn) & (t < last), lambda t: member_copy(member_by(t)).start())

    def beside():
        by_last = (member_shift == 1) & (flat > 0)

        @pl.when(by_last | later[3])
        def _():
            pl.semaphore_wait(last_in, 1)

        @pl.when(by_last)
        def _():
            member_copy(0).start()

        for k in (1, 3):
            pl.when(later[k])(side_copies[k].start)

        pl.when(below)(from_below.wait_recv)
        pl.when(above)(from_above.wait_recv)

        @pl.when(jnp.logical_not(below))
        def _():
            below_sums[...] = jnp.zeros(below_sums.shape, F32)

        @pl.when(jnp.logical_not(above))
        def _():
            above_sums[...] = jnp.zeros(above_sums.shape, F32)

        spot = iota((3 * leaves, pairs), 0)
        reads = jnp.where(spot == pairs_ref[0], 1.0, 0.0)
        reads = jnp.transpose(reads).astype(BF16)
        found = [nn(reads, part) for part in split(ext_ref[...])]
        left_side = iota((pairs, LANES), 1) < vectors
        rights = []
        for k in range(half):
            high, low = (part[:, k * LANES : (k + 1) * LANES] for part in found)
            rights.append(jnp.where(left_side, high, pltpu.roll(low, vectors, 1)))
            rights.append(jnp.where(left_side, pltpu.roll(high, vectors, 1), low))
        rights = jnp.concatenate(rights, axis=0).astype(BF16)
        for j in range(leaf_blocks):
            block = slice(j * LANES, (j + 1) * LANES)
            high_both = nn(pair_high_ref[block, :], rights)
            added = high_both[:, :vectors] + (high_both[:, vectors:] + nn(pair_low_ref[block, :], rights[:, :vectors]))
            down = local_down_ref[:, block] + jnp.transpose(added)
            cut = slice(j * width, (j + 1) * width)
            acc_ref[:, cut] = acc_ref[:, cut] + picked_by(nn, split(down), basis_blocks[j])

        pl.when(before)(from_before.wait_recv)
        pl.when(after)(from_after.wait_recv)

        @pl.when(jnp.logical_not(before))
        def _():
            left_halo[...] = jnp.zeros((vectors, halo), BF16)

        @pl.when(jnp.logical_not(after))
        def _():
            right_halo[...] = jnp.zeros((vectors, halo), BF16)

        near_part(0, 0, halo, True)
        near_part(leaves // 2 - 1, span - halo, span, True)

    def relay():
        all_members().wait_recv()
        both = three(nn, (to_group_ref[0], to_group_ref[1]), split(members_ref[...]))
        group_sum = both[:RANK, :vectors] + both[RANK:, vectors:]
        own_group[...] = side_by_side([group_sum[:HALF], group_sum[HALF:]])

        @pl.when(flat > 0)
        def _():
            each(groups, lambda t: t < group_turn, lambda t: group_copy(group_by(t)).start())

        wait(group_in, groups - 1 - group_turn)
        each(groups, lambda t: t > group_turn, lambda t: group_copy(group_by(t)).start())

        @pl.when(stand_in)
        def _():
            for j in range(1, groups):
                stand_in_copy(j).start()

    maps_work()
    late_sends()

    def stage(step, carry):
        turn = jnp.where(
            member_shift == 1, step, jnp.where(member < cores, lax.rem(step + 2, 3), jnp.where(step == 0, 0, 3 - step))
        )
        pl.when(turn == 0)(local_work)
        pl.when(turn == 1)(beside)
        pl.when(turn == 2)(relay)
        return carry

    lax.fori_loop(0, 3, stage, 0)

    def mapped(ref, first, count):
        turned_sums = jnp.transpose(ref[...])
        turned_sums = split(side_by_side([turned_sums[:vectors], turned_sums[vectors:]]))
        cut = slice(first * RANK, (first + count) * RANK)
        return three(nt, turned_sums, (map_ref[0][:, cut], map_ref[1][:, cut]))

    here_ref[...] = mapped(members_ref, 0, members)
    all_groups(group_send).wait_recv()
    down_here = here_ref[...] + mapped(groups_ref, members, groups)
    down_parts = split(down_here)
    lanes3 = iota(down_here.shape, 1)
    middle = (lanes3 >= RANK) & (lanes3 < 2 * RANK)
    down3 = jnp.where(middle, down_parts[1].astype(F32), down_parts[0].astype(F32))
    down_ref[...] = down3.astype(BF16)

    all_members().wait_send()
    pl.when(flat > 0)(all_groups(group_send).wait_send)
    pl.when(stand_in)(all_groups(stand_in_send).wait_send)
    pl.when(after)(to_after.wait_send)
    pl.when(before)(to_before.wait_send)
    pl.when(above)(to_above.wait_send)
    pl.when(below)(to_below.wait_send)


def last_part(acc_ref, final_ref, down_ref, out_ref, held_ref, sem):
    down3 = down_ref[...]
    points = out_ref.shape[1]
    width = points // 8
    for j in range(8):
        cut = slice(j * width, (j + 1) * width)
        held_ref[:, cut] = acc_ref[:, cut] + nn(down3, final_ref[:, cut])
        pltpu.make_async_copy(held_ref.at[:, cut], out_ref.at[:, cut], sem).start()
    pltpu.make_async_copy(held_ref, out_ref, sem).wait()


def split_lon(n_lon):
    members = 16 if n_lon >= 128 else 1 << n_lon.bit_length() // 2
    return n_lon // members, members


def shards(
    n_lat,
    n_lon,
    ensemble,
    leaf_basis,
    near_blocks,
    local_transfer,
    local_coupling,
    upper_transfer,
    upper_coupling,
    pair_source,
    pair_target,
    pair_coupling,
):
    vectors, points = ensemble.shape
    leaves, leaf_points, window = near_blocks.shape
    halo = window // 2 - leaf_points // 2
    groups, members = split_lon(n_lon)
    pairs = pair_source.shape[2]

    def by_node(matrices):
        nodes = matrices.shape[1]
        return jnp.transpose(matrices[0], (1, 2, 0)).reshape(RANK * RANK, nodes)

    member_blocks = max(1, 2 * members // NODES)
    group_blocks = max(1, 2 * groups // NODES)
    blocks = 2 * leaves // NODES + member_blocks + group_blocks
    upper_nodes = upper_transfer.shape[1]
    operands = (
        ensemble,
        leaf_basis,
        near_blocks,
        by_node(local_transfer),
        by_node(local_coupling),
        by_node(upper_transfer),
        by_node(upper_coupling),
        pair_source[0],
        pair_target[0],
        by_node(pair_coupling[0]),
    )
    scratch = [
        ((vectors, points + 2 * halo), BF16),
        ((RANK, points), BF16),
        (near_blocks.shape, BF16),
        ((RANK * RANK, 2 * leaves), F32),
        ((2, RANK * RANK, 2 * leaves), F32),
        ((2, RANK * RANK, upper_nodes), F32),
        ((2, 1, pairs), jnp.int32),
        ((blocks * LANES, LANES), BF16),
        ((blocks * LANES, LANES), BF16),
        ((blocks * LANES, LANES), BF16),
        ((blocks * LANES, LANES), BF16),
        ((leaves // NODES, LANES, NODES * leaf_points), BF16),
        ((vectors, (2 * leaves // NODES - 1) * LANES), F32),
        ((RANK, LANES), F32),
        ((3 * leaves, RANK * vectors), F32),
        ((members * HALF, LANES), F32),
        ((groups * HALF, LANES), F32),
        ((2, 2 * RANK, members * HALF), BF16),
        ((2, 3 * RANK, (members + groups) * RANK), BF16),
        ((vectors, leaves * RANK), F32),
        ((leaves * RANK, 2 * pairs * RANK // 2), BF16),
        ((leaves * RANK, 2 * pairs * RANK // 2), BF16),
        ((vectors, 3 * RANK), F32),
    ]
    whole = pl.BlockSpec(memory_space=pltpu.VMEM)
    kept = pl.pallas_call(
        functools.partial(kernel, (n_lat, groups, members)),
        out_shape=(
            jax.ShapeDtypeStruct((vectors, points), F32),
            jax.ShapeDtypeStruct((3 * RANK, points), BF16),
            jax.ShapeDtypeStruct((vectors, 3 * RANK), BF16),
        ),
        in_specs=[pl.BlockSpec(memory_space=pltpu.HBM)] * len(operands),
        out_specs=(whole, whole, whole),
        scratch_shapes=[pltpu.VMEM(shape, dtype) for shape, dtype in scratch]
        + [
            pltpu.SemaphoreType.DMA((7,)),
            pltpu.SemaphoreType.DMA,
            pltpu.SemaphoreType.DMA,
            pltpu.SemaphoreType.DMA,
            pltpu.SemaphoreType.DMA((4,)),
            pltpu.SemaphoreType.DMA,
            pltpu.SemaphoreType.DMA,
            pltpu.SemaphoreType.DMA((4,)),
            pltpu.SemaphoreType.REGULAR,
            pltpu.SemaphoreType.REGULAR,
            pltpu.SemaphoreType.REGULAR,
            pltpu.SemaphoreType.REGULAR,
        ],
        compiler_params=pltpu.CompilerParams(
            collective_id=0, has_side_effects=True, vmem_limit_bytes=40 * 2**20
        ),
        name="h2_tree",
    )(*[pltpu.with_memory_space_constraint(operand, pltpu.HBM) for operand in operands])
    return pl.pallas_call(
        last_part,
        out_shape=jax.ShapeDtypeStruct((vectors, points), F32),
        in_specs=[whole] * 3,
        out_specs=pl.BlockSpec(memory_space=pltpu.HBM),
        scratch_shapes=[pltpu.VMEM((vectors, points), F32), pltpu.SemaphoreType.DMA],
        compiler_params=pltpu.CompilerParams(vmem_limit_bytes=8 * 2**20),
        name="h2_last",
    )(*kept)


def solution(mesh):
    return jax.shard_map(
        functools.partial(shards, mesh.shape["lat"], mesh.shape["lon"]),
        mesh=mesh,
        in_specs=(
            P(None, ("lat", "lon")),
            P(None, ("lat", "lon")),
            P(("lat", "lon"), None, None),
            P(("lat", "lon"), None, None, None),
            P(("lat", "lon"), None, None, None),
            P("lat", None, None, None),
            P("lat", None, None, None),
            P("lat", "lon", None),
            P("lat", "lon", None),
            P("lat", "lon", None, None, None),
        ),
        out_specs=P(None, ("lat", "lon")),
        check_vma=False,
    )
```
